32 devices in a mesh: dp: 4 (over z), tensor: 8 (over y, x, core).
Axes of the slice: x: 2, y: 2, z: 4, core: 2. Of those that a mesh axis runs over, the one named last changes fastest.
Arguments:
- activations: bfloat16 [64, 8192], P('dp'), may hold values from -6 to 6
- query_weight: bfloat16 [8192, 8192], P(None, 'tensor'), may hold values from -0.0625 to 0.0625
- output_weight: bfloat16 [8192, 8192], P('tensor'), may hold values from -0.375 to 0.375
- key_cache: bfloat16 [64, 8, 1024, 128], P(('dp', 'tensor'))
- value_cache: bfloat16 [64, 8, 1024, 128], P(('dp', 'tensor')), may hold values from -6 to 6
- fresh_pair: bfloat16 [64, 2, 1024], P(('dp', 'tensor')), may hold values from -6 to 6
- cache_length: int32 [64], P(('dp', 'tensor')), may hold values from 2 to 1024
- row_tenant: int32 [64], P('dp'), may hold values from 0 to 31, as said below
- tenant_slot: int32 [32], replicated, may hold values from 0 to 31, as said below
- query_deltas: bfloat16 [32, 64, 128, 128], P('dp', 'tensor'), may hold values from -0.1796875 to 0.1796875
- query_where: int32 [32, 64], P('dp', 'tensor'), may hold values from 0 to 511, as said below
- output_deltas: bfloat16 [32, 64, 128, 128], P('dp', 'tensor'), may hold values from -0.71875 to 0.71875
- output_where: int32 [32, 64], P('dp', 'tensor'), may hold values from 0 to 511, as said below
Outputs:
- layer_out: bfloat16 [64, 8192], P('dp', 'tensor')
The draws below stay inside these ranges and needn't reach their ends.
Inputs may be any that keep to these rules, and one draw needn't show every extreme that they name: A permutation: tenant t's tiles sit in slot tenant_slot[t], on dp index tenant_slot[t] // 8. `row_tenant`: among the requests of one dp group (16 consecutive rows), at most 8 have tenants stored on one dp index; one store receives exactly 8 from every group. `query_where`: within each block of 8 entries (one slot, one shard) the places are distinct. `output_where`: within each block of 8 entries (one slot, one shard) the places are distinct.
All inputs are finite; a program needn't handle non-finite values.
Results may differ from the reference program's by a relative error of at most 0.0089.
Values may be sent and summed in bfloat16 or wider, within the bound.
A program may use at most 192 MiB of HBM per device.

```python
import jax
import jax.numpy as jnp
from jax import lax

D = 8192
H = 64
HD = 128
KVH = 8
TILE = 128
KS = 8
TEN_DEV = 8
CTX = 1024
COLS_DEV = 1024
SHARD_TILES = 512
TILE_SLOTS = 64
GROUP_ROWS = 16
ROWS = 64
STORES = 4
TENANTS = 32
CAP = 8
N_TENSOR = 8


def tenant_layout(key):
    seeded = jax.random.fold_in(key, 4242)
    key_perm, key_busy, key_groups = jax.random.split(seeded, 3)
    slot_of = jax.random.permutation(key_perm, TENANTS).astype(jnp.int32)
    owner_of = jnp.argsort(slot_of).astype(jnp.int32)
    busy_store = jax.random.randint(key_busy, (), 0, STORES, dtype=jnp.int32)

    def one_group(group_key):
        key_pool, key_mix, key_local = jax.random.split(group_key, 3)
        others = (busy_store + 1 + jnp.arange(STORES - 1, dtype=jnp.int32)) % STORES
        pooled = jnp.repeat(others, CAP)
        pooled = jax.random.permutation(key_pool, pooled)[:GROUP_ROWS - CAP]
        chosen = jnp.concatenate([jnp.full((CAP,), busy_store, dtype=jnp.int32), pooled.astype(jnp.int32)])
        chosen = jax.random.permutation(key_mix, chosen)
        local_pick = jax.random.randint(key_local, (GROUP_ROWS,), 0, TEN_DEV, dtype=jnp.int32)
        return owner_of[chosen * TEN_DEV + local_pick]
    tenants = jax.vmap(one_group)(jax.random.split(key_groups, STORES))
    return (slot_of, tenants.reshape(ROWS).astype(jnp.int32))


def draw_tenant_slot(key, part):
    return tenant_layout(key)[0]


def draw_row_tenant(key, part):
    return tenant_layout(key)[1]


def tile_places(key, salt):
    all_keys = jax.random.split(jax.random.fold_in(key, salt), TENANTS * (TILE_SLOTS // KS))
    picks = jax.vmap(lambda one_key: jax.random.permutation(one_key, SHARD_TILES)[:KS])(all_keys)
    return picks.astype(jnp.int32).reshape(TENANTS, TILE_SLOTS)


def draw_query_where(key, part):
    return tile_places(key, 101)


def draw_output_where(key, part):
    return tile_places(key, 202)


def draw_key_cache(key, part):
    values = jax.random.normal(key, (ROWS, KVH, CTX, HD), jnp.float32)
    return values.astype(jnp.bfloat16)


def set_ends(values, key, least, top_value):
    dims = values.shape
    place = [jax.random.randint(jax.random.fold_in(key, axis), (), 0, dims[axis]) for axis in range(len(dims))]
    values = values.at[tuple(place)].set(least)
    longest = dims.index(max(dims))
    place[longest] = (place[longest] + 1) % dims[longest]
    return values.at[tuple(place)].set(top_value)


def level_of(rng, shape, cuts, low, high):
    level = 1.0
    for dim, shards_of in cuts:
        steps = jax.random.uniform(jax.random.fold_in(jax.random.fold_in(rng, 6), dim), (shards_of,), jnp.float32, low / len(cuts), high / len(cuts))
        level = level * jnp.repeat(jnp.exp(steps), shape[dim] // shards_of).reshape((-1,) + (1,) * (len(shape) - 1 - dim))
    return level


def noise(key, extent, scale, most, pieces=(), kind=jnp.bfloat16):
    factor_of = level_of(key, extent, pieces, -0.22, 0.18) if pieces else 1.0
    drawn = jax.random.normal(key, extent, jnp.float32) * scale * factor_of
    return jnp.minimum(jnp.maximum(drawn, -most), most).astype(kind)


def setup_inputs(seed: int = 0) -> dict:
    keys = jax.random.split(jax.random.key(seed), 14)
    return {
        "activations": noise(keys[0], (ROWS, D), 1.0, 6.0, ((0, 4),)),
        "query_weight": noise(keys[1], (D, H * HD), D ** -0.5, 0.0625, ((1, 8),)),
        "output_weight": noise(keys[2], (H * HD, D), (H * HD // 32) ** -0.5, 0.375, ((0, 8),)),
        "key_cache": draw_key_cache(jax.random.fold_in(keys[13], 71), 0),
        "value_cache": noise(keys[4], (ROWS, KVH, CTX, HD), 1.0, 6.0, ((0, 32),)),
        "fresh_pair": noise(keys[5], (ROWS, 2, KVH * HD), 1.0, 6.0, ((0, 32),)),
        "cache_length": set_ends(jax.random.randint(keys[6], (ROWS,), 2, CTX + 1), jax.random.fold_in(keys[6], 1), 2, CTX).astype(jnp.int32),
        "row_tenant": draw_row_tenant(jax.random.fold_in(keys[13], 71), 0),
        "tenant_slot": draw_tenant_slot(jax.random.fold_in(keys[13], 71), 0),
        "query_deltas": noise(keys[9], (TENANTS, TILE_SLOTS, TILE, TILE), 0.03, 0.1796875, ((0, 4), (1, 8))),
        "query_where": draw_query_where(jax.random.fold_in(keys[13], 71), 0),
        "output_deltas": noise(keys[11], (TENANTS, TILE_SLOTS, TILE, TILE), 0.12, 0.71875, ((0, 4), (1, 8))),
        "output_where": draw_output_where(jax.random.fold_in(keys[13], 71), 0),
    }


def apply_tiles(inputs, row_slot, deltas, where_list, first_slot, out_columns):
    tile_size = deltas.shape[-1]
    slot_count = where_list.shape[0]
    per_slot = where_list.shape[1]
    out_tiles = out_columns // tile_size
    blocks = inputs.reshape(inputs.shape[0], inputs.shape[1] // tile_size, tile_size)
    flat_places = where_list.reshape(slot_count * per_slot)
    source = flat_places // out_tiles
    target = flat_places % out_tiles
    picked = jnp.take(blocks, source, axis=1)
    owners = first_slot + jnp.arange(slot_count * per_slot, dtype=jnp.int32) // per_slot
    chosen = row_slot[:, None] == owners[None, :]
    picked = jnp.where(chosen[:, :, None], picked, jnp.zeros((), inputs.dtype))
    products = jnp.einsum("rkt,kts->rks", picked.astype(jnp.float32), deltas.reshape(slot_count * per_slot, tile_size, tile_size).astype(jnp.float32))
    spread = (target[:, None] == jnp.arange(out_tiles, dtype=jnp.int32)[None, :]).astype(jnp.float32)
    combined = jnp.einsum("rks,kb->rbs", products, spread, precision=lax.Precision.HIGHEST)
    return combined.reshape(inputs.shape[0], out_columns)


def attend(query_rows, key_cache, value_cache, fresh_pair, cache_length):
    count_rows, kv_heads, context, head_dim = key_cache.shape
    grouped = query_rows.reshape(count_rows, kv_heads, -1, head_dim).astype(jnp.float32)
    score_scale = head_dim ** -0.5
    scores = jnp.einsum("rkgd,rkld->rkgl", grouped, key_cache.astype(jnp.float32)) * score_scale
    fresh_key = fresh_pair[:, 0].reshape(count_rows, kv_heads, head_dim).astype(jnp.float32)
    fresh_value = fresh_pair[:, 1].reshape(count_rows, kv_heads, head_dim).astype(jnp.float32)
    own_score = jnp.einsum("rkgd,rkd->rkg", grouped, fresh_key) * score_scale
    position = jnp.arange(context, dtype=jnp.int32)
    visible = (position[None, :] < cache_length[:, None])[:, None, None, :]
    scores = jnp.where(visible, scores, -1e30)
    highest = jnp.maximum(jnp.max(scores, axis=3), own_score)
    weights = jnp.where(visible, jnp.exp(scores - highest[..., None]), 0.0)
    own_weight = jnp.exp(own_score - highest)
    denominator = jnp.sum(weights, axis=3) + own_weight
    probabilities = (weights / denominator[..., None]).astype(jnp.bfloat16)
    own_probability = (own_weight / denominator).astype(jnp.bfloat16)
    mixed = jnp.einsum("rkgl,rkld->rkgd", probabilities.astype(jnp.float32), value_cache.astype(jnp.float32))
    mixed = mixed + own_probability.astype(jnp.float32)[..., None] * fresh_value[:, :, None, :]
    return mixed.astype(jnp.bfloat16).reshape(count_rows, -1)


def reference(activations, query_weight, output_weight, key_cache, value_cache, fresh_pair, cache_length, row_tenant, tenant_slot, query_deltas, query_where, output_deltas, output_where):
    row_slot = jnp.take(tenant_slot, row_tenant)
    query_parts = []
    for shard_index in range(N_TENSOR):
        query_parts.append(apply_tiles(activations, row_slot, query_deltas[:, shard_index * KS:(shard_index + 1) * KS], query_where[:, shard_index * KS:(shard_index + 1) * KS], 0, COLS_DEV))
    query_extra = jnp.concatenate(query_parts, axis=1)
    query_heads = (jnp.dot(activations, query_weight, preferred_element_type=jnp.float32) + query_extra).astype(jnp.bfloat16)
    attended = attend(query_heads, key_cache, value_cache, fresh_pair, cache_length)
    out_extra = jnp.zeros((activations.shape[0], D), jnp.float32)
    for shard_index in range(N_TENSOR):
        heads_part = attended[:, shard_index * COLS_DEV:(shard_index + 1) * COLS_DEV]
        out_extra = out_extra + apply_tiles(heads_part, row_slot, output_deltas[:, shard_index * KS:(shard_index + 1) * KS], output_where[:, shard_index * KS:(shard_index + 1) * KS], 0, D)
    layer_out = jnp.dot(attended, output_weight, preferred_element_type=jnp.float32) + out_extra
    return layer_out.astype(jnp.bfloat16)
```

```python
import functools

import jax
import jax.numpy as jnp
from jax import lax
from jax.experimental import pallas as pl
from jax.experimental.pallas import tpu as pltpu
from jax.sharding import PartitionSpec as P

LANES = 128
CAP = 8
F32 = jnp.float32
BF16 = jnp.bfloat16


def kernel(
    dims,
    act_ref,
    fresh_ref,
    length_ref,
    tenant_ref,
    table_ref,
    qwhere_ref,
    owhere_ref,
    qw_hbm,
    ow_hbm,
    key_hbm,
    value_hbm,
    qd_hbm,
    od_hbm,
    out_ref,
    qw,
    ow,
    keys,
    values,
    qd,
    od,
    info,
    acc,
    pack_out,
    pack_in,
    back_out,
    back_in,
    head_rows,
    q_out,
    q_in,
    extra_out,
    extra_in,
    a_out,
    a_in,
    part,
    sum_out,
    sum_in,
    qw_sem,
    ow_sem,
    cache_sem,
    delta_sem,
    dp_send,
    dp_recv,
    tp_send,
    tp_recv,
    all_send,
    all_recv,
):
    stores, shards, group, rows, width, tiles, slots, context = dims
    heads = width // LANES
    all_tiles = act_ref.shape[1] // LANES
    half = tiles // 2
    dp = lax.axis_index("dp")
    tp = lax.axis_index("tensor")
    chunk = qw.shape[0] // shards
    message = a_out.dtype
    compact = stores * CAP

    def peer_of(axis, step):
        me, count = (dp, stores) if axis == "dp" else (tp, shards)
        return lax.rem(me + step, count)

    qd_copy = pltpu.make_async_copy(qd_hbm, qd, delta_sem.at[0])
    od_copy = pltpu.make_async_copy(od_hbm, od, delta_sem.at[1])
    key_copy = pltpu.make_async_copy(key_hbm, keys, cache_sem.at[0])
    value_copy = pltpu.make_async_copy(value_hbm, values, cache_sem.at[1])

    def qw_copy(c):
        span = pl.ds(pl.multiple_of(c * chunk, chunk), chunk)
        return pltpu.make_async_copy(qw_hbm.at[span], qw.at[span], qw_sem.at[c])

    def ow_copy(c):
        span = pl.ds(pl.multiple_of(c * width, width), width)
        return pltpu.make_async_copy(ow_hbm.at[:, span], ow.at[c], ow_sem.at[c])

    def start_all(copy):
        def step(c, carry):
            copy(c).start()
            return carry

        lax.fori_loop(0, shards, step, 0)

    barrier = pltpu.get_barrier_semaphore()
    for far in range(stores):
        for step in range(shards):
            if far or step:
                pl.semaphore_signal(
                    barrier,
                    inc=1,
                    device_id={"dp": peer_of("dp", far), "tensor": peer_of("tensor", step)},
                    device_id_type=pl.DeviceIdType.MESH,
                )
    start_all(qw_copy)
    qd_copy.start()

    lane = lax.broadcasted_iota(jnp.int32, (group, LANES), 1)
    row = lax.broadcasted_iota(jnp.int32, (group, LANES), 0)
    slot = jnp.zeros((group, LANES), jnp.int32)
    for r in range(group):
        slot = jnp.where(row == r, table_ref[tenant_ref[r]], slot)
    info[dp] = jnp.zeros(info.shape[1:], jnp.int32)
    info[dp, 0:slots, 0:tiles] = qwhere_ref[...]
    info[dp, 0:slots, tiles : 2 * tiles] = owhere_ref[...]
    info[dp, slots : slots + group, :] = slot
    acc[...] = jnp.zeros_like(acc)
    pl.semaphore_wait(barrier, stores * shards - 1)

    def send(axis, phase, step, src, dst):
        sems = (dp_send, dp_recv) if axis == "dp" else (tp_send, tp_recv)
        copy = pltpu.make_async_remote_copy(
            src_ref=src,
            dst_ref=dst,
            send_sem=sems[0].at[phase, step],
            recv_sem=sems[1].at[phase, step],
            device_id={axis: peer_of(axis, step)},
            device_id_type=pl.DeviceIdType.MESH,
        )
        copy.start()
        return copy

    sent = []

    def exchange(axis, phase, src, dst):
        me, count = (dp, stores) if axis == "dp" else (tp, shards)
        copies = [
            send(axis, phase, step, src(peer_of(axis, step)), dst.at[me])
            for step in range(1, count)
        ]
        sent.extend(copies)
        return copies

    def scatter(phase, src, dst, steps, over):
        copies = []
        for step in steps:
            peer = peer_of("tensor", step)
            for far in reversed(range(over)):
                if step == 0 and far == 0:
                    continue
                to = peer_of("dp", far)
                copy = pltpu.make_async_remote_copy(
                    src_ref=src(to, peer),
                    dst_ref=dst.at[dp, tp],
                    send_sem=all_send.at[phase, far, step],
                    recv_sem=all_recv.at[phase, far, step],
                    device_id={"dp": to, "tensor": peer},
                    device_id_type=pl.DeviceIdType.MESH,
                )
                copy.start()
                copies.append(copy)
        sent.extend(copies)
        return copies

    def arrive(copies):
        for copy in copies:
            copy.wait_recv()

    info_copies = exchange("dp", 0, lambda peer: info.at[dp], info)

    def base_query(first, last):
        def step(c, carry):
            qw_copy(c).wait()
            span = pl.ds(pl.multiple_of(c * chunk, chunk), chunk)
            acc[...] += jnp.dot(act_ref[:, span], qw[span, :], preferred_element_type=F32)
            return carry

        lax.fori_loop(first, last, step, 0)

    store = jnp.zeros((group, LANES), jnp.int32)
    for index in range(1, stores):
        store = store + jnp.where(slot >= index * slots, 1, 0)
    of_store = lane == store
    row_i = lax.broadcasted_iota(jnp.int32, (group, group), 0)
    row_j = lax.broadcasted_iota(jnp.int32, (group, group), 1)
    earlier = jnp.where(row_j < row_i, 1.0, 0.0).astype(F32)
    rank = jnp.dot(earlier, jnp.where(of_store, 1.0, 0.0).astype(F32), preferred_element_type=F32)
    rank = jnp.sum(jnp.where(of_store, rank, 0.0), axis=1, keepdims=True)
    place = store.astype(F32) * CAP + rank
    home = jnp.where(lane.astype(F32) == place, 1.0, 0.0).astype(F32)
    home = home[:, : stores * CAP]
    outward = home.T.astype(BF16)
    homeward = home.astype(BF16)

    def pack(picked, out):
        packed = jnp.dot(outward, jnp.concatenate(picked, axis=1), preferred_element_type=F32)
        packed = packed.reshape(stores, CAP, tiles * LANES)
        low = packed[:, :, : half * LANES]
        high = packed[:, :, half * LANES :]
        out[...] = jnp.concatenate([low, high], axis=1).astype(BF16)

    def products(taken, deltas):
        results = []
        for k in range(tiles):
            x = jnp.concatenate([jnp.where(m, taken[k], 0.0) for m in own_slot], axis=1)
            w = deltas[:, k].reshape(slots * LANES, LANES)
            results.append(jnp.dot(x.astype(BF16), w, preferred_element_type=F32))
        return results

    def returned(back):
        got = back[...].astype(F32)
        low = got[:, :CAP].reshape(stores * CAP, half * LANES)
        high = got[:, CAP:].reshape(stores * CAP, half * LANES)
        rows_in = jnp.concatenate([low, high], axis=1).astype(BF16)
        return jnp.dot(homeward, rows_in, preferred_element_type=F32)

    def spread(terms, targets, column):
        total = jnp.where(targets[0] == column, terms[0], 0.0)
        for k in range(1, tiles):
            total += jnp.where(targets[k] == column, terms[k], 0.0)
        return total

    def lanes_of(table, k):
        return jnp.broadcast_to(table[:, k : k + 1], table.shape)

    base_query(0, shards // 4)
    key_copy.start()
    value_copy.start()

    arrive(info_copies)
    where = jnp.zeros((group, LANES), jnp.int32)
    for d in range(stores):
        for s in range(slots):
            where = where + jnp.where(slot == d * slots + s, info[d, s : s + 1, :], 0)
    q_place = [lanes_of(where, k) for k in range(tiles)]
    o_place = [lanes_of(where, tiles + k) for k in range(tiles)]
    head_shift = heads.bit_length() - 1
    tile_shift = all_tiles.bit_length() - 1
    q_source = [lax.shift_right_logical(p, head_shift) for p in q_place]
    o_target = [p & (all_tiles - 1) for p in o_place]

    picked = [jnp.zeros((group, LANES), F32) for _ in range(tiles)]
    for t in range(all_tiles):
        block = act_ref[:, t * LANES : (t + 1) * LANES].astype(F32)
        picked = [jnp.where(q_source[k] == t, block, picked[k]) for k in range(tiles)]
    pack([p.astype(BF16) for p in picked], pack_out)
    pack_in[dp] = pack_out[dp]
    pack_copies = exchange("dp", 1, lambda peer: pack_out.at[peer], pack_in)

    picks = []
    marks = []
    for g in range(stores):
        theirs = info[g, slots : slots + group, :]
        mine = (theirs >= dp * slots) & (theirs < (dp + 1) * slots)
        before = jnp.dot(earlier, jnp.where(mine, 1.0, 0.0), preferred_element_type=F32)
        pick = mine & (lane.astype(F32) == before + g * CAP)
        picks.append(jnp.where(pick, 1.0, 0.0))
        marks.append((theirs - dp * slots + 1).astype(F32))
    expand = jnp.concatenate(picks, axis=0)[:, :compact]
    gather = expand.T
    mark = jnp.dot(gather, jnp.concatenate(marks, axis=0), preferred_element_type=F32)
    expand = expand.astype(BF16)
    gather = gather.astype(BF16)
    own_slot = [mark == s + 1 for s in range(slots)]
    near = jnp.zeros((compact, LANES), jnp.int32)
    for s in range(slots):
        near = near + jnp.where(own_slot[s], info[dp, s : s + 1, :], 0)
    near_target = [lanes_of(near, k) & (heads - 1) for k in range(tiles)]
    near_source = [
        lax.shift_right_logical(lanes_of(near, tiles + k), tile_shift) for k in range(tiles)
    ]

    base_query(shards // 4, shards)
    od_copy.start()
    start_all(ow_copy)
    for h in range(heads):
        head_rows[dp, :, h, :] = acc[:, h * LANES : (h + 1) * LANES]
    q_out[...] = head_rows[dp].reshape(shards, rows * heads, LANES)
    q_in[tp] = q_out[tp]
    q_copies = exchange("tensor", 0, lambda peer: q_out.at[peer], q_in)

    qd_copy.wait()
    arrive(pack_copies)
    got = pack_in[...].astype(F32)
    taken = []
    for k in range(tiles):
        start = CAP * (k // half)
        column = (k % half) * LANES
        x = got[:, start : start + CAP, column : column + LANES]
        taken.append(x.reshape(compact, LANES))
    terms = products(taken, qd)
    placed = jnp.concatenate([spread(terms, near_target, h) for h in range(heads)], axis=1)
    placed = jnp.dot(expand, placed.astype(BF16), preferred_element_type=F32)
    placed = placed.reshape(stores, group, width)
    for h in range(heads):
        head_rows[:, :, h, :] = placed[:, :, h * LANES : (h + 1) * LANES]
    extra = head_rows[...].reshape(stores, shards, rows * heads, LANES)
    extra_out[...] = extra.astype(BF16).astype(message)
    extra_in[dp, tp] = extra_out[dp, tp]
    extra_copies = scatter(
        0, lambda to, peer: extra_out.at[to, peer], extra_in, range(shards), stores
    )

    scale = LANES ** (-0.5)
    lines = rows * heads
    line = lax.broadcasted_iota(jnp.int32, (lines, 1), 0)
    of_row = [(line >= r * heads) & (line < (r + 1) * heads) for r in range(rows)]
    limit = jnp.zeros((lines, 1), jnp.int32)
    for r in range(rows):
        limit = jnp.where(of_row[r], length_ref[r], limit)
    visible = lax.broadcasted_iota(jnp.int32, (lines, context), 1) < limit
    kv_heads = keys.shape[1]

    key_copy.wait()
    value_copy.wait()
    arrive(q_copies)
    arrive(extra_copies)

    def attend(step):
        j = peer_of("tensor", step)
        g = j * kv_heads // shards
        q32 = q_in[j]
        for d in range(stores):
            q32 = q32 + extra_in[d, j].astype(F32)
        q = q32.astype(BF16)
        q32 = q.astype(F32)
        fresh_key = jnp.zeros((lines, LANES), F32)
        fresh_value = jnp.zeros((lines, LANES), F32)
        scores = None
        for r in range(rows):
            here = pl.ds(pl.multiple_of(g * LANES, LANES), LANES)
            fresh = fresh_ref[r, :, here].astype(F32)
            fresh_key = jnp.where(of_row[r], fresh[0:1], fresh_key)
            fresh_value = jnp.where(of_row[r], fresh[1:2], fresh_value)
            one = lax.dot_general(
                q, keys[r, g], (((1,), (1,)), ((), ())), preferred_element_type=F32
            )
            scores = one if scores is None else jnp.where(of_row[r], one, scores)
        own = jnp.sum(q32 * fresh_key, axis=1, keepdims=True) * scale
        scores = jnp.where(visible, scores * scale, -1e30)
        highest = jnp.maximum(jnp.max(scores, axis=1, keepdims=True), own)
        weights = jnp.where(visible, jnp.exp(scores - highest), 0.0)
        own_weight = jnp.exp(own - highest)
        inverse = 1.0 / (jnp.sum(weights, axis=1, keepdims=True) + own_weight)
        chance = (weights * inverse).astype(BF16)
        own_chance = (own_weight * inverse).astype(BF16).astype(F32)
        mixed = None
        for r in range(rows):
            one = jnp.dot(chance, values[r, g], preferred_element_type=F32)
            mixed = one if mixed is None else jnp.where(of_row[r], one, mixed)
        mixed = mixed + own_chance * fresh_value
        a_out[j] = mixed.astype(BF16).astype(message)

    a_copies = []
    parts = [range(0, shards // 2), range(shards // 2, shards)]
    for steps in parts:
        for step in steps:
            attend(step)
        a_copies += scatter(1, lambda to, peer: a_out.at[peer], a_in, steps, stores)
    a_in[dp, tp] = a_out[tp]
    arrive(a_copies)
    head_rows[...] = a_in[...].astype(F32).reshape(stores, group, heads, LANES)
    blocks = [head_rows[:, :, h, :].reshape(stores * group, LANES) for h in range(heads)]
    blocks = jnp.concatenate([b.astype(BF16) for b in blocks], axis=1)
    blocks = jnp.dot(gather, blocks, preferred_element_type=F32)
    taken = []
    for k in range(tiles):
        one = jnp.zeros((compact, LANES), F32)
        for h in range(heads):
            one = jnp.where(near_source[k] == h, blocks[:, h * LANES : (h + 1) * LANES], one)
        taken.append(one)
    od_copy.wait()
    terms = products(taken, od)
    low = jnp.concatenate(terms[:half], axis=1).reshape(stores, CAP, half * LANES)
    high = jnp.concatenate(terms[half:], axis=1).reshape(stores, CAP, half * LANES)
    back_out[...] = jnp.concatenate([low, high], axis=1).astype(BF16)
    back_in[dp] = back_out[dp]
    back_copies = exchange("dp", 2, lambda peer: back_out.at[peer], back_in)
    attended = jnp.concatenate([head_rows[dp, :, h, :].astype(BF16) for h in range(heads)], axis=1)

    def base_out(first, last):
        def step(c, carry):
            ow_copy(c).wait()
            part[c] = jnp.dot(attended, ow[c], preferred_element_type=F32)
            return carry

        lax.fori_loop(first, last, step, 0)

    base_out(0, shards)
    arrive(back_copies)
    terms = returned(back_in)
    terms = [terms[:, k * LANES : (k + 1) * LANES] for k in range(tiles)]

    def whole_part(owner):
        extra = [spread(terms, o_target, owner * heads + h) for h in range(heads)]
        return part[owner] + jnp.concatenate(extra, axis=1)

    sum_copies = []
    for step in range(1, shards):
        owner = peer_of("tensor", step)
        sum_out[step] = whole_part(owner).astype(BF16)
        sum_copies.append(send("tensor", 1, step, sum_out.at[step], sum_in.at[step]))
    sent.extend(sum_copies)
    total = whole_part(tp)
    for step in range(1, shards):
        sum_copies[step - 1].wait_recv()
        total = total + sum_in[step].astype(F32)
    out_ref[...] = total.astype(BF16)
    for copy in sent:
        copy.wait_send()


def body(
    activations,
    query_weight,
    output_weight,
    key_cache,
    value_cache,
    fresh_pair,
    cache_length,
    row_tenant,
    tenant_slot,
    query_deltas,
    query_where,
    output_deltas,
    output_where,
):
    stores = lax.axis_size("dp")
    shards = lax.axis_size("tensor")
    group = activations.shape[0]
    rows = key_cache.shape[0]
    width = query_weight.shape[1]
    slots, tiles = query_where.shape
    context = key_cache.shape[2]
    heads = width // LANES
    lines = rows * heads
    message = BF16 if lines % 16 == 0 else F32
    dims = (stores, shards, group, rows, width, tiles, slots, context)
    pack_shape = (stores, 2 * CAP, tiles // 2 * LANES)
    all_shape = (stores, shards, lines, LANES)
    vmem = pl.BlockSpec(memory_space=pltpu.VMEM)
    smem = pl.BlockSpec(memory_space=pltpu.SMEM)
    anywhere = pl.BlockSpec(memory_space=pl.ANY)
    return pl.pallas_call(
        functools.partial(kernel, dims),
        out_shape=jax.ShapeDtypeStruct((group, width), BF16),
        in_specs=[vmem, vmem, smem, smem, smem, vmem, vmem] + [anywhere] * 6,
        out_specs=vmem,
        scratch_shapes=[
            pltpu.VMEM(query_weight.shape, BF16),
            pltpu.VMEM((shards, width, width), BF16),
            pltpu.VMEM(key_cache.shape, BF16),
            pltpu.VMEM(value_cache.shape, BF16),
            pltpu.VMEM(query_deltas.shape, BF16),
            pltpu.VMEM(output_deltas.shape, BF16),
            pltpu.VMEM((stores, slots + group, LANES), jnp.int32),
            pltpu.VMEM((group, width), F32),
            pltpu.VMEM(pack_shape, BF16),
            pltpu.VMEM(pack_shape, BF16),
            pltpu.VMEM(pack_shape, BF16),
            pltpu.VMEM(pack_shape, BF16),
            pltpu.VMEM((stores, group, heads, LANES), F32),
            pltpu.VMEM((shards, lines, LANES), F32),
            pltpu.VMEM((shards, lines, LANES), F32),
            pltpu.VMEM(all_shape, message),
            pltpu.VMEM(all_shape, message),
            pltpu.VMEM((shards, lines, LANES), message),
            pltpu.VMEM(all_shape, message),
            pltpu.VMEM((shards, group, width), F32),
            pltpu.VMEM((shards, group, width), BF16),
            pltpu.VMEM((shards, group, width), BF16),
            pltpu.SemaphoreType.DMA((shards,)),
            pltpu.SemaphoreType.DMA((shards,)),
            pltpu.SemaphoreType.DMA((2,)),
            pltpu.SemaphoreType.DMA((2,)),
            pltpu.SemaphoreType.DMA((3, stores)),
            pltpu.SemaphoreType.DMA((3, stores)),
            pltpu.SemaphoreType.DMA((2, shards)),
            pltpu.SemaphoreType.DMA((2, shards)),
            pltpu.SemaphoreType.DMA((2, stores, shards)),
            pltpu.SemaphoreType.DMA((2, stores, shards)),
        ],
        compiler_params=pltpu.CompilerParams(
            collective_id=0, has_side_effects=True, vmem_limit_bytes=56 * 1024 * 1024
        ),
        name="decode_layer",
    )(
        activations,
        fresh_pair,
        cache_length,
        row_tenant,
        tenant_slot,
        query_where,
        output_where,
        query_weight,
        output_weight,
        key_cache,
        value_cache,
        query_deltas,
        output_deltas,
    )


def solution(mesh):
    placed = (
        P("dp", None),
        P(None, "tensor"),
        P("tensor", None),
        P(("dp", "tensor"), None, None, None),
        P(("dp", "tensor"), None, None, None),
        P(("dp", "tensor"), None, None),
        P(("dp", "tensor")),
        P("dp"),
        P(),
        P("dp", "tensor", None, None),
        P("dp", "tensor"),
        P("dp", "tensor", None, None),
        P("dp", "tensor"),
    )
    return jax.shard_map(
        body, mesh=mesh, in_specs=placed, out_specs=P("dp", "tensor"), check_vma=False
    )
```

```python
import functools

import jax
import jax.numpy as jnp
from jax import lax
from jax.experimental import pallas as pl
from jax.experimental.pallas import tpu as pltpu
from jax.sharding import PartitionSpec as P

LANES = 128
CAP = 8
F32 = jnp.float32
BF16 = jnp.bfloat16


def kernel(
    dims,
    act_ref,
    fresh_ref,
    length_ref,
    tenant_ref,
    table_ref,
    qwhere_ref,
    owhere_ref,
    qw_hbm,
    ow_hbm,
    key_hbm,
    value_hbm,
    qd_hbm,
    od_hbm,
    out_ref,
    qw,
    ow,
    keys,
    values,
    qd,
    od,
    info,
    acc,
    pack_out,
    pack_in,
    back_out,
    back_in,
    head_rows,
    q_out,
    q_in,
    extra_out,
    extra_in,
    a_out,
    a_in,
    part,
    sum_out,
    sum_in,
    qw_sem,
    ow_sem,
    cache_sem,
    delta_sem,
    dp_send,
    dp_recv,
    tp_send,
    tp_recv,
    all_send,
    all_recv,
):
    stores, shards, group, rows, width, tiles, slots, context = dims
    heads = width // LANES
    all_tiles = act_ref.shape[1] // LANES
    half = tiles // 2
    dp = lax.axis_index("dp")
    tp = lax.axis_index("tensor")
    chunk = qw.shape[0] // shards
    message = a_out.dtype
    compact = stores * CAP

    peers = {
        "dp": [dp] + [lax.rem(dp + step, stores) for step in range(1, stores)],
        "tensor": [tp] + [lax.rem(tp + step, shards) for step in range(1, shards)],
    }

    def peer_of(axis, step):
        return peers[axis][step]

    qd_copy = pltpu.make_async_copy(qd_hbm, qd, delta_sem.at[0])
    od_copy = pltpu.make_async_copy(od_hbm, od, delta_sem.at[1])
    key_copy = pltpu.make_async_copy(key_hbm, keys, cache_sem.at[0])
    value_copy = pltpu.make_async_copy(value_hbm, values, cache_sem.at[1])

    def qw_copy(c):
        span = pl.ds(pl.multiple_of(c * chunk, chunk), chunk)
        return pltpu.make_async_copy(qw_hbm.at[span], qw.at[span], qw_sem.at[c])

    def ow_copy(c):
        span = pl.ds(pl.multiple_of(c * width, width), width)
        return pltpu.make_async_copy(ow_hbm.at[:, span], ow.at[c], ow_sem.at[c])

    def start_all(copy):
        def step(c, carry):
            copy(c).start()
            return carry

        lax.fori_loop(0, shards, step, 0)

    barrier = pltpu.get_barrier_semaphore()
    for axis in ("dp", "tensor"):
        for peer in peers[axis][1:]:
            pl.semaphore_signal(
                barrier, inc=1, device_id={axis: peer}, device_id_type=pl.DeviceIdType.MESH
            )
    start_all(qw_copy)
    qd_copy.start()

    lane = lax.broadcasted_iota(jnp.int32, (group, LANES), 1)
    row = lax.broadcasted_iota(jnp.int32, (group, LANES), 0)
    slot = jnp.zeros((group, LANES), jnp.int32)
    for r in range(group):
        slot = jnp.where(row == r, table_ref[tenant_ref[r]], slot)
    info[dp] = jnp.zeros(info.shape[1:], jnp.int32)
    info[dp, 0:slots, 0:tiles] = qwhere_ref[...]
    info[dp, 0:slots, tiles : 2 * tiles] = owhere_ref[...]
    info[dp, slots : slots + group, :] = slot
    acc[...] = jnp.zeros_like(acc)
    pl.semaphore_wait(barrier, stores - 1 + shards - 1)

    def send(axis, phase, step, src, dst):
        sems = (dp_send, dp_recv) if axis == "dp" else (tp_send, tp_recv)
        copy = pltpu.make_async_remote_copy(
            src_ref=src,
            dst_ref=dst,
            send_sem=sems[0].at[phase, step],
            recv_sem=sems[1].at[phase, step],
            device_id={axis: peer_of(axis, step)},
            device_id_type=pl.DeviceIdType.MESH,
        )
        copy.start()
        return copy

    sent = []

    def exchange(axis, phase, src, dst):
        me, count = (dp, stores) if axis == "dp" else (tp, shards)
        copies = [
            send(axis, phase, step, src(peer_of(axis, step)), dst.at[me])
            for step in range(1, count)
        ]
        sent.extend(copies)
        return copies

    def scatter(phase, src, dst, steps):
        copies = {}
        for step in steps:
            peer = peer_of("tensor", step)
            for far in reversed(range(stores)):
                if step == 0 and far == 0:
                    continue
                to = peer_of("dp", far)
                copy = pltpu.make_async_remote_copy(
                    src_ref=src(to, peer),
                    dst_ref=dst.at[dp, tp],
                    send_sem=all_send.at[phase, far, step],
                    recv_sem=all_recv.at[phase, far, step],
                    device_id={"dp": to, "tensor": peer},
                    device_id_type=pl.DeviceIdType.MESH,
                )
                copy.start()
                copies[far, step] = copy
        sent.extend(copies.values())
        return copies

    def arrive(copies):
        for copy in copies:
            copy.wait_recv()

    info_copies = exchange("dp", 0, lambda peer: info.at[dp], info)

    def base_query(first, last):
        def step(c, carry):
            qw_copy(c).wait()
            span = pl.ds(pl.multiple_of(c * chunk, chunk), chunk)
            acc[...] += jnp.dot(act_ref[:, span], qw[span, :], preferred_element_type=F32)
            return carry

        lax.fori_loop(first, last, step, 0)

    store = jnp.zeros((group, LANES), jnp.int32)
    for index in range(1, stores):
        store = store + jnp.where(slot >= index * slots, 1, 0)
    of_store = lane == store
    row_i = lax.broadcasted_iota(jnp.int32, (group, group), 0)
    row_j = lax.broadcasted_iota(jnp.int32, (group, group), 1)
    earlier = jnp.where(row_j < row_i, 1.0, 0.0).astype(F32)
    rank = jnp.dot(earlier, jnp.where(of_store, 1.0, 0.0).astype(F32), preferred_element_type=F32)
    rank = jnp.sum(jnp.where(of_store, rank, 0.0), axis=1, keepdims=True)
    place = store.astype(F32) * CAP + rank
    home = jnp.where(lane.astype(F32) == place, 1.0, 0.0).astype(F32)
    home = home[:, : stores * CAP]
    outward = home.T.astype(BF16)
    homeward = home.astype(BF16)

    def pack(picked, out):
        packed = jnp.dot(outward, jnp.concatenate(picked, axis=1), preferred_element_type=F32)
        packed = packed.reshape(stores, CAP, tiles * LANES)
        low = packed[:, :, : half * LANES]
        high = packed[:, :, half * LANES :]
        out[...] = jnp.concatenate([low, high], axis=1).astype(BF16)

    def products(taken, deltas):
        results = []
        for k in range(tiles):
            x = jnp.concatenate([jnp.where(m, taken[k], 0.0) for m in own_slot], axis=1)
            w = deltas[:, k].reshape(slots * LANES, LANES)
            results.append(jnp.dot(x.astype(BF16), w, preferred_element_type=F32))
        return results

    def returned(back):
        got = back[...].astype(F32)
        low = got[:, :CAP].reshape(stores * CAP, half * LANES)
        high = got[:, CAP:].reshape(stores * CAP, half * LANES)
        rows_in = jnp.concatenate([low, high], axis=1).astype(BF16)
        return jnp.dot(homeward, rows_in, preferred_element_type=F32)

    def spread(terms, targets, column):
        total = jnp.where(targets[0] == column, terms[0], 0.0)
        for k in range(1, tiles):
            total += jnp.where(targets[k] == column, terms[k], 0.0)
        return total

    def lanes_of(table, k):
        return jnp.broadcast_to(table[:, k : k + 1], table.shape)

    base_query(0, shards // 4)
    key_copy.start()
    value_copy.start()

    arrive(info_copies)
    where = jnp.zeros((group, LANES), jnp.int32)
    for d in range(stores):
        for s in range(slots):
            where = where + jnp.where(slot == d * slots + s, info[d, s : s + 1, :], 0)
    q_place = [lanes_of(where, k) for k in range(tiles)]
    o_place = [lanes_of(where, tiles + k) for k in range(tiles)]
    head_shift = heads.bit_length() - 1
    tile_shift = all_tiles.bit_length() - 1
    q_source = [lax.shift_right_logical(p, head_shift) for p in q_place]
    o_target = [p & (all_tiles - 1) for p in o_place]

    picked = [jnp.zeros((group, LANES), F32) for _ in range(tiles)]
    for t in range(all_tiles):
        block = act_ref[:, t * LANES : (t + 1) * LANES].astype(F32)
        picked = [jnp.where(q_source[k] == t, block, picked[k]) for k in range(tiles)]
    pack([p.astype(BF16) for p in picked], pack_out)
    pack_in[dp] = pack_out[dp]
    pack_copies = exchange("dp", 1, lambda peer: pack_out.at[peer], pack_in)

    picks = []
    marks = []
    for g in range(stores):
        theirs = info[g, slots : slots + group, :]
        mine = (theirs >= dp * slots) & (theirs < (dp + 1) * slots)
        before = jnp.dot(earlier, jnp.where(mine, 1.0, 0.0), preferred_element_type=F32)
        pick = mine & (lane.astype(F32) == before + g * CAP)
        picks.append(jnp.where(pick, 1.0, 0.0))
        marks.append((theirs - dp * slots + 1).astype(F32))
    expand = jnp.concatenate(picks, axis=0)[:, :compact]
    gather = expand.T
    mark = jnp.dot(gather, jnp.concatenate(marks, axis=0), preferred_element_type=F32)
    expand = expand.astype(BF16)
    gather = gather.astype(BF16)
    own_slot = [mark == s + 1 for s in range(slots)]
    near = jnp.zeros((compact, LANES), jnp.int32)
    for s in range(slots):
        near = near + jnp.where(own_slot[s], info[dp, s : s + 1, :], 0)
    near_target = [lanes_of(near, k) & (heads - 1) for k in range(tiles)]
    near_source = [
        lax.shift_right_logical(lanes_of(near, tiles + k), tile_shift) for k in range(tiles)
    ]

    base_query(shards // 4, shards)
    od_copy.start()
    start_all(ow_copy)
    for h in range(heads):
        head_rows[dp, :, h, :] = acc[:, h * LANES : (h + 1) * LANES]
    q_out[...] = head_rows[dp].reshape(shards, rows * heads, LANES)
    q_in[tp] = q_out[tp]
    q_copies = exchange("tensor", 0, lambda peer: q_out.at[peer], q_in)

    qd_copy.wait()
    arrive(pack_copies)
    got = pack_in[...].astype(F32)
    taken = []
    for k in range(tiles):
        start = CAP * (k // half)
        column = (k % half) * LANES
        x = got[:, start : start + CAP, column : column + LANES]
        taken.append(x.reshape(compact, LANES))
    terms = products(taken, qd)
    placed = jnp.concatenate([spread(terms, near_target, h) for h in range(heads)], axis=1)
    placed = jnp.dot(expand, placed.astype(BF16), preferred_element_type=F32)
    placed = placed.reshape(stores, group, width)
    for h in range(heads):
        head_rows[:, :, h, :] = placed[:, :, h * LANES : (h + 1) * LANES]
    extra = head_rows[...].reshape(stores, shards, rows * heads, LANES)
    extra_out[...] = extra.astype(BF16).astype(message)
    extra_in[dp, tp] = extra_out[dp, tp]
    order = [0] + list(range(shards - 1, 0, -1))
    extra_copies = scatter(
        0, lambda to, peer: extra_out.at[to, peer], extra_in, range(shards)
    )

    scale = LANES ** (-0.5)
    lines = rows * heads
    line = lax.broadcasted_iota(jnp.int32, (lines, 1), 0)
    of_row = [(line >= r * heads) & (line < (r + 1) * heads) for r in range(rows)]
    limit = jnp.zeros((lines, 1), jnp.int32)
    for r in range(rows):
        limit = jnp.where(of_row[r], length_ref[r], limit)
    visible = lax.broadcasted_iota(jnp.int32, (lines, context), 1) < limit
    kv_heads = keys.shape[1]

    key_copy.wait()
    value_copy.wait()
    arrive(q_copies)

    def attend(step):
        j = peer_of("tensor", step)
        g = j * kv_heads // shards
        q32 = q_in[j]
        for d in range(stores):
            q32 = q32 + extra_in[d, j].astype(F32)
        q = q32.astype(BF16)
        q32 = q.astype(F32)
        fresh_key = jnp.zeros((lines, LANES), F32)
        fresh_value = jnp.zeros((lines, LANES), F32)
        scores = None
        for r in range(rows):
            here = pl.ds(pl.multiple_of(g * LANES, LANES), LANES)
            fresh = fresh_ref[r, :, here].astype(F32)
            fresh_key = jnp.where(of_row[r], fresh[0:1], fresh_key)
            fresh_value = jnp.where(of_row[r], fresh[1:2], fresh_value)
            one = lax.dot_general(
                q, keys[r, g], (((1,), (1,)), ((), ())), preferred_element_type=F32
            )
            scores = one if scores is None else jnp.where(of_row[r], one, scores)
        own = jnp.sum(q32 * fresh_key, axis=1, keepdims=True) * scale
        scores = jnp.where(visible, scores * scale, -1e30)
        highest = jnp.maximum(jnp.max(scores, axis=1, keepdims=True), own)
        weights = jnp.where(visible, jnp.exp(scores - highest), 0.0)
        own_weight = jnp.exp(own - highest)
        inverse = 1.0 / (jnp.sum(weights, axis=1, keepdims=True) + own_weight)
        chance = (weights * inverse).astype(BF16)
        own_chance = (own_weight * inverse).astype(BF16).astype(F32)
        mixed = None
        for r in range(rows):
            one = jnp.dot(chance, values[r, g], preferred_element_type=F32)
            mixed = one if mixed is None else jnp.where(of_row[r], one, mixed)
        mixed = mixed + own_chance * fresh_value
        a_out[j] = mixed.astype(BF16).astype(message)

    a_copies = {}
    for steps in (order[: shards // 2], order[shards // 2 :]):
        for step in steps:
            source = (shards - step) % shards
            arrive([extra_copies[far, source] for far in range(stores) if far or source])
        for step in steps:
            attend(step)
        a_copies.update(scatter(1, lambda to, peer: a_out.at[peer], a_in, steps))
    a_in[dp, tp] = a_out[tp]

    def base_out(first, last):
        def step(c, carry):
            ow_copy(c).wait()
            part[c] = jnp.dot(attended, ow[c], preferred_element_type=F32)
            return carry

        lax.fori_loop(first, last, step, 0)

    arrive([copy for (far, step), copy in a_copies.items() if far == 0])
    head_rows[dp] = a_in[dp].astype(F32).reshape(group, heads, LANES)
    attended = jnp.concatenate([head_rows[dp, :, h, :].astype(BF16) for h in range(heads)], axis=1)
    base_out(0, shards // 2)
    arrive([copy for (far, step), copy in a_copies.items() if far > 0])
    head_rows[...] = a_in[...].astype(F32).reshape(stores, group, heads, LANES)
    blocks = [head_rows[:, :, h, :].reshape(stores * group, LANES) for h in range(heads)]
    blocks = jnp.concatenate([b.astype(BF16) for b in blocks], axis=1)
    blocks = jnp.dot(gather, blocks, preferred_element_type=F32)
    taken = []
    for k in range(tiles):
        one = jnp.zeros((compact, LANES), F32)
        for h in range(heads):
            one = jnp.where(near_source[k] == h, blocks[:, h * LANES : (h + 1) * LANES], one)
        taken.append(one)
    od_copy.wait()
    terms = products(taken, od)
    low = jnp.concatenate(terms[:half], axis=1).reshape(stores, CAP, half * LANES)
    high = jnp.concatenate(terms[half:], axis=1).reshape(stores, CAP, half * LANES)
    back_out[...] = jnp.concatenate([low, high], axis=1).astype(BF16)
    back_in[dp] = back_out[dp]
    back_copies = exchange("dp", 2, lambda peer: back_out.at[peer], back_in)
    base_out(shards // 2, shards)
    for copy in sent:
        copy.wait_send()
    arrive(back_copies)
    terms = returned(back_in)
    terms = [terms[:, k * LANES : (k + 1) * LANES] for k in range(tiles)]

    def whole_part(owner):
        extra = [spread(terms, o_target, owner * heads + h) for h in range(heads)]
        return part[owner] + jnp.concatenate(extra, axis=1)

    sum_copies = []
    for step in range(1, shards):
        owner = peer_of("tensor", step)
        sum_out[step] = whole_part(owner).astype(BF16)
        sum_copies.append(send("tensor", 1, step, sum_out.at[step], sum_in.at[step]))
    total = whole_part(tp)
    for step in range(1, shards):
        sum_copies[step - 1].wait_recv()
        total = total + sum_in[step].astype(F32)
    out_ref[...] = total.astype(BF16)
    for copy in sum_copies:
        copy.wait_send()


def body(
    activations,
    query_weight,
    output_weight,
    key_cache,
    value_cache,
    fresh_pair,
    cache_length,
    row_tenant,
    tenant_slot,
    query_deltas,
    query_where,
    output_deltas,
    output_where,
):
    stores = lax.axis_size("dp")
    shards = lax.axis_size("tensor")
    group = activations.shape[0]
    rows = key_cache.shape[0]
    width = query_weight.shape[1]
    slots, tiles = query_where.shape
    context = key_cache.shape[2]
    heads = width // LANES
    lines = rows * heads
    message = BF16 if lines % 16 == 0 else F32
    dims = (stores, shards, group, rows, width, tiles, slots, context)
    pack_shape = (stores, 2 * CAP, tiles // 2 * LANES)
    all_shape = (stores, shards, lines, LANES)
    vmem = pl.BlockSpec(memory_space=pltpu.VMEM)
    smem = pl.BlockSpec(memory_space=pltpu.SMEM)
    anywhere = pl.BlockSpec(memory_space=pl.ANY)
    return pl.pallas_call(
        functools.partial(kernel, dims),
        out_shape=jax.ShapeDtypeStruct((group, width), BF16),
        in_specs=[vmem, vmem, smem, smem, smem, vmem, vmem] + [anywhere] * 6,
        out_specs=vmem,
        scratch_shapes=[
            pltpu.VMEM(query_weight.shape, BF16),
            pltpu.VMEM((shards, width, width), BF16),
            pltpu.VMEM(key_cache.shape, BF16),
            pltpu.VMEM(value_cache.shape, BF16),
            pltpu.VMEM(query_deltas.shape, BF16),
            pltpu.VMEM(output_deltas.shape, BF16),
            pltpu.VMEM((stores, slots + group, LANES), jnp.int32),
            pltpu.VMEM((group, width), F32),
            pltpu.VMEM(pack_shape, BF16),
            pltpu.VMEM(pack_shape, BF16),
            pltpu.VMEM(pack_shape, BF16),
            pltpu.VMEM(pack_shape, BF16),
            pltpu.VMEM((stores, group, heads, LANES), F32),
            pltpu.VMEM((shards, lines, LANES), F32),
            pltpu.VMEM((shards, lines, LANES), F32),
            pltpu.VMEM(all_shape, message),
            pltpu.VMEM(all_shape, message),
            pltpu.VMEM((shards, lines, LANES), message),
            pltpu.VMEM(all_shape, message),
            pltpu.VMEM((shards, group, width), F32),
            pltpu.VMEM((shards, group, width), BF16),
            pltpu.VMEM((shards, group, width), BF16),
            pltpu.SemaphoreType.DMA((shards,)),
            pltpu.SemaphoreType.DMA((shards,)),
            pltpu.SemaphoreType.DMA((2,)),
            pltpu.SemaphoreType.DMA((2,)),
            pltpu.SemaphoreType.DMA((3, stores)),
            pltpu.SemaphoreType.DMA((3, stores)),
            pltpu.SemaphoreType.DMA((2, shards)),
            pltpu.SemaphoreType.DMA((2, shards)),
            pltpu.SemaphoreType.DMA((2, stores, shards)),
            pltpu.SemaphoreType.DMA((2, stores, shards)),
        ],
        compiler_params=pltpu.CompilerParams(
            collective_id=0, has_side_effects=True, vmem_limit_bytes=56 * 1024 * 1024
        ),
        name="decode_layer",
    )(
        activations,
        fresh_pair,
        cache_length,
        row_tenant,
        tenant_slot,
        query_where,
        output_where,
        query_weight,
        output_weight,
        key_cache,
        value_cache,
        query_deltas,
        output_deltas,
    )


def solution(mesh):
    placed = (
        P("dp", None),
        P(None, "tensor"),
        P("tensor", None),
        P(("dp", "tensor"), None, None, None),
        P(("dp", "tensor"), None, None, None),
        P(("dp", "tensor"), None, None),
        P(("dp", "tensor")),
        P("dp"),
        P(),
        P("dp", "tensor", None, None),
        P("dp", "tensor"),
        P("dp", "tensor", None, None),
        P("dp", "tensor"),
    )
    return jax.shard_map(
        body, mesh=mesh, in_specs=placed, out_specs=P("dp", "tensor"), check_vma=False
    )
```

```python
import functools

import jax
import jax.numpy as jnp
from jax import lax
from jax.experimental import pallas as pl
from jax.experimental.pallas import tpu as pltpu
from jax.sharding import PartitionSpec as P

LANES = 128
CAP = 8
F32 = jnp.float32
BF16 = jnp.bfloat16


def kernel(
    dims,
    act_ref,
    fresh_ref,
    length_ref,
    tenant_ref,
    table_ref,
    qwhere_ref,
    owhere_ref,
    qw_hbm,
    ow_hbm,
    key_hbm,
    value_hbm,
    qd_hbm,
    od_hbm,
    out_ref,
    qw,
    ow,
    keys,
    values,
    qd,
    od,
    info,
    acc,
    pack_out,
    pack_in,
    back_out,
    back_in,
    head_rows,
    q_out,
    q_in,
    extra_out,
    extra_in,
    a_out,
    a_in,
    part,
    sum_out,
    sum_in,
    qw_sem,
    ow_sem,
    cache_sem,
    delta_sem,
    dp_send,
    dp_recv,
    tp_send,
    tp_recv,
    all_send,
    all_recv,
    pair_out,
    pair_in,
    pair_send,
    pair_recv,
):
    stores, shards, group, rows, width, tiles, slots, context = dims
    heads = width // LANES
    all_tiles = act_ref.shape[1] // LANES
    half = tiles // 2
    dp = lax.axis_index("dp")
    tp = lax.axis_index("tensor")
    chunk = qw.shape[0] // shards
    message = a_out.dtype
    compact = stores * CAP
    half_width = width // 2
    parity = lax.rem(dp, 2)
    partner = dp + 1 - 2 * parity

    peers = {
        "dp": [dp] + [lax.rem(dp + step, stores) for step in range(1, stores)],
        "tensor": [tp] + [lax.rem(tp + step, shards) for step in range(1, shards)],
    }

    def peer_of(axis, step):
        return peers[axis][step]

    qd_copy = pltpu.make_async_copy(qd_hbm, qd, delta_sem.at[0])
    od_copy = pltpu.make_async_copy(od_hbm, od, delta_sem.at[1])
    key_copy = pltpu.make_async_copy(key_hbm, keys, cache_sem.at[0])
    value_copy = pltpu.make_async_copy(value_hbm, values, cache_sem.at[1])

    def qw_copy(c):
        span = pl.ds(pl.multiple_of(c * chunk, chunk), chunk)
        return pltpu.make_async_copy(qw_hbm.at[span], qw.at[span], qw_sem.at[c])

    def ow_copy(c):
        owner = lax.rem(tp + c, shards)
        start = owner * width + parity * half_width
        span = pl.ds(pl.multiple_of(start, half_width), half_width)
        return pltpu.make_async_copy(ow_hbm.at[:, span], ow.at[c], ow_sem.at[c])

    def start_all(copy):
        def step(c, carry):
            copy(c).start()
            return carry

        lax.fori_loop(0, shards, step, 0)

    barrier = pltpu.get_barrier_semaphore()
    for axis in ("dp", "tensor"):
        for peer in peers[axis][1:]:
            pl.semaphore_signal(
                barrier, inc=1, device_id={axis: peer}, device_id_type=pl.DeviceIdType.MESH
            )
    start_all(qw_copy)
    qd_copy.start()

    lane = lax.broadcasted_iota(jnp.int32, (group, LANES), 1)
    row = lax.broadcasted_iota(jnp.int32, (group, LANES), 0)
    slot = jnp.zeros((group, LANES), jnp.int32)
    for r in range(group):
        slot = jnp.where(row == r, table_ref[tenant_ref[r]], slot)
    info[dp] = jnp.zeros(info.shape[1:], jnp.int32)
    info[dp, 0:slots, 0:tiles] = qwhere_ref[...]
    info[dp, 0:slots, tiles : 2 * tiles] = owhere_ref[...]
    info[dp, slots : slots + group, :] = slot
    acc[...] = jnp.zeros_like(acc)
    pl.semaphore_wait(barrier, stores - 1 + shards - 1)

    def send(axis, phase, step, src, dst):
        sems = (dp_send, dp_recv) if axis == "dp" else (tp_send, tp_recv)
        copy = pltpu.make_async_remote_copy(
            src_ref=src,
            dst_ref=dst,
            send_sem=sems[0].at[phase, step],
            recv_sem=sems[1].at[phase, step],
            device_id={axis: peer_of(axis, step)},
            device_id_type=pl.DeviceIdType.MESH,
        )
        copy.start()
        return copy

    sent = []

    def exchange(axis, phase, src, dst):
        me, count = (dp, stores) if axis == "dp" else (tp, shards)
        copies = [
            send(axis, phase, step, src(peer_of(axis, step)), dst.at[me])
            for step in range(1, count)
        ]
        sent.extend(copies)
        return copies

    def scatter(phase, src, dst, steps):
        copies = {}
        for step in steps:
            peer = peer_of("tensor", step)
            for far in reversed(range(stores)):
                if step == 0 and far == 0:
                    continue
                to = peer_of("dp", far)
                copy = pltpu.make_async_remote_copy(
                    src_ref=src(to, peer),
                    dst_ref=dst.at[dp, tp],
                    send_sem=all_send.at[phase, far, step],
                    recv_sem=all_recv.at[phase, far, step],
                    device_id={"dp": to, "tensor": peer},
                    device_id_type=pl.DeviceIdType.MESH,
                )
                copy.start()
                copies[far, step] = copy
        sent.extend(copies.values())
        return copies

    def arrive(copies):
        for copy in copies:
            copy.wait_recv()

    info_copies = exchange("dp", 0, lambda peer: info.at[dp], info)

    def base_query(first, last):
        def step(c, carry):
            qw_copy(c).wait()
            span = pl.ds(pl.multiple_of(c * chunk, chunk), chunk)
            acc[...] += jnp.dot(act_ref[:, span], qw[span, :], preferred_element_type=F32)
            return carry

        lax.fori_loop(first, last, step, 0)

    store = jnp.zeros((group, LANES), jnp.int32)
    for index in range(1, stores):
        store = store + jnp.where(slot >= index * slots, 1, 0)
    of_store = lane == store
    row_i = lax.broadcasted_iota(jnp.int32, (group, group), 0)
    row_j = lax.broadcasted_iota(jnp.int32, (group, group), 1)
    earlier = jnp.where(row_j < row_i, 1.0, 0.0).astype(F32)
    rank = jnp.dot(earlier, jnp.where(of_store, 1.0, 0.0).astype(F32), preferred_element_type=F32)
    rank = jnp.sum(jnp.where(of_store, rank, 0.0), axis=1, keepdims=True)
    place = store.astype(F32) * CAP + rank
    home = jnp.where(lane.astype(F32) == place, 1.0, 0.0).astype(F32)
    home = home[:, : stores * CAP]
    outward = home.T.astype(BF16)
    homeward = home.astype(BF16)

    def pack(picked, out):
        packed = jnp.dot(outward, jnp.concatenate(picked, axis=1), preferred_element_type=F32)
        packed = packed.reshape(stores, CAP, tiles * LANES)
        low = packed[:, :, : half * LANES]
        high = packed[:, :, half * LANES :]
        out[...] = jnp.concatenate([low, high], axis=1).astype(BF16)

    def products(taken, deltas):
        results = []
        for k in range(tiles):
            x = jnp.concatenate([jnp.where(m, taken[k], 0.0) for m in own_slot], axis=1)
            w = deltas[:, k].reshape(slots * LANES, LANES)
            results.append(jnp.dot(x.astype(BF16), w, preferred_element_type=F32))
        return results

    def returned(back):
        got = back[...].astype(F32)
        low = got[:, :CAP].reshape(stores * CAP, half * LANES)
        high = got[:, CAP:].reshape(stores * CAP, half * LANES)
        rows_in = jnp.concatenate([low, high], axis=1).astype(BF16)
        return jnp.dot(homeward, rows_in, preferred_element_type=F32)

    def spread(terms, targets, column):
        total = jnp.where(targets[0] == column, terms[0], 0.0)
        for k in range(1, tiles):
            total += jnp.where(targets[k] == column, terms[k], 0.0)
        return total

    def lanes_of(table, k):
        return jnp.broadcast_to(table[:, k : k + 1], table.shape)

    base_query(0, shards // 4)
    key_copy.start()
    value_copy.start()

    arrive(info_copies)
    where = jnp.zeros((group, LANES), jnp.int32)
    for d in range(stores):
        for s in range(slots):
            where = where + jnp.where(slot == d * slots + s, info[d, s : s + 1, :], 0)
    q_place = [lanes_of(where, k) for k in range(tiles)]
    o_place = [lanes_of(where, tiles + k) for k in range(tiles)]
    head_shift = heads.bit_length() - 1
    tile_shift = all_tiles.bit_length() - 1
    q_source = [lax.shift_right_logical(p, head_shift) for p in q_place]
    o_target = [p & (all_tiles - 1) for p in o_place]

    picked = [jnp.zeros((group, LANES), F32) for _ in range(tiles)]
    for t in range(all_tiles):
        block = act_ref[:, t * LANES : (t + 1) * LANES].astype(F32)
        picked = [jnp.where(q_source[k] == t, block, picked[k]) for k in range(tiles)]
    pack([p.astype(BF16) for p in picked], pack_out)
    pack_in[dp] = pack_out[dp]
    pack_copies = exchange("dp", 1, lambda peer: pack_out.at[peer], pack_in)

    picks = []
    marks = []
    for g in range(stores):
        theirs = info[g, slots : slots + group, :]
        mine = (theirs >= dp * slots) & (theirs < (dp + 1) * slots)
        before = jnp.dot(earlier, jnp.where(mine, 1.0, 0.0), preferred_element_type=F32)
        pick = mine & (lane.astype(F32) == before + g * CAP)
        picks.append(jnp.where(pick, 1.0, 0.0))
        marks.append((theirs - dp * slots + 1).astype(F32))
    expand = jnp.concatenate(picks, axis=0)[:, :compact]
    gather = expand.T
    mark = jnp.dot(gather, jnp.concatenate(marks, axis=0), preferred_element_type=F32)
    expand = expand.astype(BF16)
    gather = gather.astype(BF16)
    own_slot = [mark == s + 1 for s in range(slots)]
    near = jnp.zeros((compact, LANES), jnp.int32)
    for s in range(slots):
        near = near + jnp.where(own_slot[s], info[dp, s : s + 1, :], 0)
    near_target = [lanes_of(near, k) & (heads - 1) for k in range(tiles)]
    near_source = [
        lax.shift_right_logical(lanes_of(near, tiles + k), tile_shift) for k in range(tiles)
    ]

    base_query(shards // 4, 3 * shards // 4)
    od_copy.start()
    start_all(ow_copy)

    qd_copy.wait()
    arrive(pack_copies)
    got = pack_in[...].astype(F32)
    taken = []
    for k in range(tiles):
        start = CAP * (k // half)
        column = (k % half) * LANES
        x = got[:, start : start + CAP, column : column + LANES]
        taken.append(x.reshape(compact, LANES))
    terms = products(taken, qd)
    placed = jnp.concatenate([spread(terms, near_target, h) for h in range(heads)], axis=1)
    placed = jnp.dot(expand, placed.astype(BF16), preferred_element_type=F32)
    placed = placed.reshape(stores, group, width)
    for h in range(heads):
        head_rows[:, :, h, :] = placed[:, :, h * LANES : (h + 1) * LANES]
    extra = head_rows[...].reshape(stores, shards, rows * heads, LANES)
    extra_out[...] = extra.astype(BF16).astype(message)
    extra_in[dp, tp] = extra_out[dp, tp]
    order = [0] + list(range(shards - 1, 0, -1))
    extra_copies = scatter(
        0, lambda to, peer: extra_out.at[to, peer], extra_in, range(shards)
    )

    base_query(3 * shards // 4, shards)
    for h in range(heads):
        head_rows[dp, :, h, :] = acc[:, h * LANES : (h + 1) * LANES]
    q_out[...] = head_rows[dp].reshape(shards, rows * heads, LANES)
    q_in[tp] = q_out[tp]
    q_copies = exchange("tensor", 0, lambda peer: q_out.at[peer], q_in)

    scale = LANES ** (-0.5)
    lines = rows * heads
    line = lax.broadcasted_iota(jnp.int32, (lines, 1), 0)
    of_row = [(line >= r * heads) & (line < (r + 1) * heads) for r in range(rows)]
    limit = jnp.zeros((lines, 1), jnp.int32)
    for r in range(rows):
        limit = jnp.where(of_row[r], length_ref[r], limit)
    visible = lax.broadcasted_iota(jnp.int32, (lines, context), 1) < limit
    kv_heads = keys.shape[1]

    key_copy.wait()
    value_copy.wait()
    arrive(q_copies)

    def attend(step):
        j = peer_of("tensor", step)
        g = j * kv_heads // shards
        q32 = q_in[j]
        for d in range(stores):
            q32 = q32 + extra_in[d, j].astype(F32)
        q = q32.astype(BF16)
        q32 = q.astype(F32)
        fresh_key = jnp.zeros((lines, LANES), F32)
        fresh_value = jnp.zeros((lines, LANES), F32)
        scores = None
        for r in range(rows):
            here = pl.ds(pl.multiple_of(g * LANES, LANES), LANES)
            fresh = fresh_ref[r, :, here].astype(F32)
            fresh_key = jnp.where(of_row[r], fresh[0:1], fresh_key)
            fresh_value = jnp.where(of_row[r], fresh[1:2], fresh_value)
            one = lax.dot_general(
                q, keys[r, g], (((1,), (1,)), ((), ())), preferred_element_type=F32
            )
            scores = one if scores is None else jnp.where(of_row[r], one, scores)
        own = jnp.sum(q32 * fresh_key, axis=1, keepdims=True) * scale
        scores = jnp.where(visible, scores * scale, -1e30)
        highest = jnp.maximum(jnp.max(scores, axis=1, keepdims=True), own)
        weights = jnp.where(visible, jnp.exp(scores - highest), 0.0)
        own_weight = jnp.exp(own - highest)
        inverse = 1.0 / (jnp.sum(weights, axis=1, keepdims=True) + own_weight)
        chance = (weights * inverse).astype(BF16)
        own_chance = (own_weight * inverse).astype(BF16).astype(F32)
        mixed = None
        for r in range(rows):
            one = jnp.dot(chance, values[r, g], preferred_element_type=F32)
            mixed = one if mixed is None else jnp.where(of_row[r], one, mixed)
        mixed = mixed + own_chance * fresh_value
        a_out[j] = mixed.astype(BF16).astype(message)

    a_copies = {}
    for steps in (order[: shards // 2], order[shards // 2 :]):
        for step in steps:
            source = (shards - step) % shards
            arrive([extra_copies[far, source] for far in range(stores) if far or source])
        for step in steps:
            attend(step)
        a_copies.update(scatter(1, lambda to, peer: a_out.at[peer], a_in, steps))
    a_in[dp, tp] = a_out[tp]

    def pair_copy(c):
        return pltpu.make_async_remote_copy(
            src_ref=pair_out.at[c],
            dst_ref=pair_in.at[c],
            send_sem=pair_send.at[c],
            recv_sem=pair_recv.at[c],
            device_id={"dp": partner, "tensor": lax.rem(tp + c, shards)},
            device_id_type=pl.DeviceIdType.MESH,
        )

    def base_out():
        def step(c, carry):
            ow_copy(c).wait()
            both = jnp.dot(attended, ow[c], preferred_element_type=F32)
            part[c] = both.reshape(2, group, half_width)
            pair_out[c] = part[c, 1 - parity].astype(BF16)
            pair_copy(c).start()
            return carry

        lax.fori_loop(0, shards, step, 0)

    arrive(list(a_copies.values()))
    head_rows[...] = a_in[...].astype(F32).reshape(stores, group, heads, LANES)
    blocks = [head_rows[:, :, h, :].reshape(stores * group, LANES) for h in range(heads)]
    blocks = jnp.concatenate([b.astype(BF16) for b in blocks], axis=1)
    blocks = jnp.dot(gather, blocks, preferred_element_type=F32)
    taken = []
    for k in range(tiles):
        one = jnp.zeros((compact, LANES), F32)
        for h in range(heads):
            one = jnp.where(near_source[k] == h, blocks[:, h * LANES : (h + 1) * LANES], one)
        taken.append(one)
    od_copy.wait()
    terms = products(taken, od)
    low = jnp.concatenate(terms[:half], axis=1).reshape(stores, CAP, half * LANES)
    high = jnp.concatenate(terms[half:], axis=1).reshape(stores, CAP, half * LANES)
    back_out[...] = jnp.concatenate([low, high], axis=1).astype(BF16)
    back_in[dp] = back_out[dp]
    back_copies = exchange("dp", 2, lambda peer: back_out.at[peer], back_in)
    pair = pl.ds(dp - parity, 2)
    attended = [head_rows[pair, :, h, :].reshape(2 * group, LANES) for h in range(heads)]
    attended = jnp.concatenate([a.astype(BF16) for a in attended], axis=1)
    base_out()
    for copy in sent:
        copy.wait_send()
    arrive(back_copies)
    terms = returned(back_in)
    terms = [terms[:, k * LANES : (k + 1) * LANES] for k in range(tiles)]

    low_half = (1 - parity).astype(F32)
    high_half = parity.astype(F32)

    def whole_part(step):
        owner = peer_of("tensor", step)
        extra = [spread(terms, o_target, owner * heads + h) for h in range(heads)]
        base = part[step, parity]
        return jnp.concatenate(extra, axis=1) + jnp.concatenate(
            [base * low_half, base * high_half], axis=1
        )

    sum_copies = []
    for step in range(1, shards):
        sum_out[step] = whole_part(step).astype(BF16)
        sum_copies.append(send("tensor", 1, step, sum_out.at[step], sum_in.at[step]))
    total = whole_part(0)
    others = jnp.zeros((group, half_width), F32)
    for c in range(shards):
        pair_copy(c).wait_recv()
        others = others + pair_in[c].astype(F32)
    total = total + jnp.concatenate([others * high_half, others * low_half], axis=1)
    for step in range(1, shards):
        sum_copies[step - 1].wait_recv()
        total = total + sum_in[step].astype(F32)
    out_ref[...] = total.astype(BF16)
    for copy in sum_copies:
        copy.wait_send()
    for c in range(shards):
        pair_copy(c).wait_send()


def body(
    activations,
    query_weight,
    output_weight,
    key_cache,
    value_cache,
    fresh_pair,
    cache_length,
    row_tenant,
    tenant_slot,
    query_deltas,
    query_where,
    output_deltas,
    output_where,
):
    stores = lax.axis_size("dp")
    shards = lax.axis_size("tensor")
    group = activations.shape[0]
    rows = key_cache.shape[0]
    width = query_weight.shape[1]
    slots, tiles = query_where.shape
    context = key_cache.shape[2]
    heads = width // LANES
    lines = rows * heads
    message = BF16 if lines % 16 == 0 else F32
    dims = (stores, shards, group, rows, width, tiles, slots, context)
    pack_shape = (stores, 2 * CAP, tiles // 2 * LANES)
    all_shape = (stores, shards, lines, LANES)
    vmem = pl.BlockSpec(memory_space=pltpu.VMEM)
    smem = pl.BlockSpec(memory_space=pltpu.SMEM)
    anywhere = pl.BlockSpec(memory_space=pl.ANY)
    return pl.pallas_call(
        functools.partial(kernel, dims),
        out_shape=jax.ShapeDtypeStruct((group, width), BF16),
        in_specs=[vmem, vmem, smem, smem, smem, vmem, vmem] + [anywhere] * 6,
        out_specs=vmem,
        scratch_shapes=[
            pltpu.VMEM(query_weight.shape, BF16),
            pltpu.VMEM((shards, width, width // 2), BF16),
            pltpu.VMEM(key_cache.shape, BF16),
            pltpu.VMEM(value_cache.shape, BF16),
            pltpu.VMEM(query_deltas.shape, BF16),
            pltpu.VMEM(output_deltas.shape, BF16),
            pltpu.VMEM((stores, slots + group, LANES), jnp.int32),
            pltpu.VMEM((group, width), F32),
            pltpu.VMEM(pack_shape, BF16),
            pltpu.VMEM(pack_shape, BF16),
            pltpu.VMEM(pack_shape, BF16),
            pltpu.VMEM(pack_shape, BF16),
            pltpu.VMEM((stores, group, heads, LANES), F32),
            pltpu.VMEM((shards, lines, LANES), F32),
            pltpu.VMEM((shards, lines, LANES), F32),
            pltpu.VMEM(all_shape, message),
            pltpu.VMEM(all_shape, message),
            pltpu.VMEM((shards, lines, LANES), message),
            pltpu.VMEM(all_shape, message),
            pltpu.VMEM((shards, 2, group, width // 2), F32),
            pltpu.VMEM((shards, group, width), BF16),
            pltpu.VMEM((shards, group, width), BF16),
            pltpu.SemaphoreType.DMA((shards,)),
            pltpu.SemaphoreType.DMA((shards,)),
            pltpu.SemaphoreType.DMA((2,)),
            pltpu.SemaphoreType.DMA((2,)),
            pltpu.SemaphoreType.DMA((3, stores)),
            pltpu.SemaphoreType.DMA((3, stores)),
            pltpu.SemaphoreType.DMA((2, shards)),
            pltpu.SemaphoreType.DMA((2, shards)),
            pltpu.SemaphoreType.DMA((2, stores, shards)),
            pltpu.SemaphoreType.DMA((2, stores, shards)),
            pltpu.VMEM((shards, group, width // 2), BF16),
            pltpu.VMEM((shards, group, width // 2), BF16),
            pltpu.SemaphoreType.DMA((shards,)),
            pltpu.SemaphoreType.DMA((shards,)),
        ],
        compiler_params=pltpu.CompilerParams(
            collective_id=0, has_side_effects=True, vmem_limit_bytes=56 * 1024 * 1024
        ),
        name="decode_layer",
    )(
        activations,
        fresh_pair,
        cache_length,
        row_tenant,
        tenant_slot,
        query_where,
        output_where,
        query_weight,
        output_weight,
        key_cache,
        value_cache,
        query_deltas,
        output_deltas,
    )


def solution(mesh):
    placed = (
        P("dp", None),
        P(None, "tensor"),
        P("tensor", None),
        P(("dp", "tensor"), None, None, None),
        P(("dp", "tensor"), None, None, None),
        P(("dp", "tensor"), None, None),
        P(("dp", "tensor")),
        P("dp"),
        P(),
        P("dp", "tensor", None, None),
        P("dp", "tensor"),
        P("dp", "tensor", None, None),
        P("dp", "tensor"),
    )
    return jax.shard_map(
        body, mesh=mesh, in_specs=placed, out_specs=P("dp", "tensor"), check_vma=False
    )
```

```python
import functools

import jax
import jax.numpy as jnp
from jax import lax
from jax.experimental import pallas as pl
from jax.experimental.pallas import tpu as pltpu
from jax.sharding import PartitionSpec as P

LANES = 128
CAP = 8
F32 = jnp.float32
BF16 = jnp.bfloat16


def kernel(
    dims,
    act_ref,
    fresh_ref,
    length_ref,
    tenant_ref,
    table_ref,
    qwhere_ref,
    owhere_ref,
    qw_hbm,
    ow_hbm,
    key_hbm,
    value_hbm,
    qd_hbm,
    od_hbm,
    out_ref,
    qw,
    ow,
    keys,
    values,
    qd,
    od,
    info,
    acc,
    pack_out,
    pack_in,
    back_out,
    back_in,
    head_rows,
    q_out,
    q_in,
    extra_out,
    extra_in,
    a_out,
    a_in,
    part,
    sum_out,
    sum_in,
    qw_sem,
    ow_sem,
    cache_sem,
    delta_sem,
    dp_send,
    dp_recv,
    tp_send,
    tp_recv,
    all_send,
    all_recv,
    pair_out,
    pair_in,
    pair_send,
    pair_recv,
):
    stores, shards, group, rows, width, tiles, slots, context = dims
    heads = width // LANES
    all_tiles = act_ref.shape[1] // LANES
    half = tiles // 2
    dp = lax.axis_index("dp")
    tp = lax.axis_index("tensor")
    chunk = qw.shape[0] // shards
    message = a_out.dtype
    compact = stores * CAP
    half_width = width // 2
    parity = lax.rem(dp, 2)
    partner = dp + 1 - 2 * parity

    peers = {
        "dp": [dp] + [lax.rem(dp + step, stores) for step in range(1, stores)],
        "tensor": [tp] + [lax.rem(tp + step, shards) for step in range(1, shards)],
    }

    def peer_of(axis, step):
        return peers[axis][step]

    qd_copy = pltpu.make_async_copy(qd_hbm, qd, delta_sem.at[0])
    od_copy = pltpu.make_async_copy(od_hbm, od, delta_sem.at[1])
    key_copy = pltpu.make_async_copy(key_hbm, keys, cache_sem.at[0])
    value_copy = pltpu.make_async_copy(value_hbm, values, cache_sem.at[1])

    def qw_copy(c):
        span = pl.ds(pl.multiple_of(c * chunk, chunk), chunk)
        return pltpu.make_async_copy(qw_hbm.at[span], qw.at[span], qw_sem.at[c])

    def ow_copy(c):
        owner = lax.rem(tp + c, shards)
        start = owner * width + parity * half_width
        span = pl.ds(pl.multiple_of(start, half_width), half_width)
        return pltpu.make_async_copy(ow_hbm.at[:, span], ow.at[c], ow_sem.at[c])

    def start_all(copy):
        def step(c, carry):
            copy(c).start()
            return carry

        lax.fori_loop(0, shards, step, 0)

    barrier = pltpu.get_barrier_semaphore()
    for axis in ("dp", "tensor"):
        for peer in peers[axis][1:]:
            pl.semaphore_signal(
                barrier, inc=1, device_id={axis: peer}, device_id_type=pl.DeviceIdType.MESH
            )
    start_all(qw_copy)
    qd_copy.start()

    lane = lax.broadcasted_iota(jnp.int32, (group, LANES), 1)
    row = lax.broadcasted_iota(jnp.int32, (group, LANES), 0)
    slot = jnp.zeros((group, LANES), jnp.int32)
    for r in range(group):
        slot = jnp.where(row == r, table_ref[tenant_ref[r]], slot)
    info[dp] = jnp.zeros(info.shape[1:], jnp.int32)
    info[dp, 0:slots, 0:tiles] = qwhere_ref[...]
    info[dp, 0:slots, tiles : 2 * tiles] = owhere_ref[...]
    info[dp, slots : slots + group, :] = slot
    acc[...] = jnp.zeros_like(acc)
    pl.semaphore_wait(barrier, stores - 1 + shards - 1)

    def send(axis, phase, step, src, dst):
        sems = (dp_send, dp_recv) if axis == "dp" else (tp_send, tp_recv)
        copy = pltpu.make_async_remote_copy(
            src_ref=src,
            dst_ref=dst,
            send_sem=sems[0].at[phase, step],
            recv_sem=sems[1].at[phase, step],
            device_id={axis: peer_of(axis, step)},
            device_id_type=pl.DeviceIdType.MESH,
        )
        copy.start()
        return copy

    sent = []

    def exchange(axis, phase, src, dst):
        me, count = (dp, stores) if axis == "dp" else (tp, shards)
        copies = [
            send(axis, phase, step, src(peer_of(axis, step)), dst.at[me])
            for step in range(1, count)
        ]
        sent.extend(copies)
        return copies

    def scatter(phase, src, dst, steps):
        copies = {}
        for step in steps:
            peer = peer_of("tensor", step)
            for far in reversed(range(stores)):
                if step == 0 and far == 0:
                    continue
                to = peer_of("dp", far)
                copy = pltpu.make_async_remote_copy(
                    src_ref=src(to, peer),
                    dst_ref=dst.at[dp, tp],
                    send_sem=all_send.at[phase, far, step],
                    recv_sem=all_recv.at[phase, far, step],
                    device_id={"dp": to, "tensor": peer},
                    device_id_type=pl.DeviceIdType.MESH,
                )
                copy.start()
                copies[far, step] = copy
        sent.extend(copies.values())
        return copies

    def arrive(copies):
        for copy in copies:
            copy.wait_recv()

    info_copies = exchange("dp", 0, lambda peer: info.at[dp], info)

    def base_query(first, last):
        def step(c, carry):
            qw_copy(c).wait()
            span = pl.ds(pl.multiple_of(c * chunk, chunk), chunk)
            acc[...] += jnp.dot(act_ref[:, span], qw[span, :], preferred_element_type=F32)
            return carry

        lax.fori_loop(first, last, step, 0)

    store = jnp.zeros((group, LANES), jnp.int32)
    for index in range(1, stores):
        store = store + jnp.where(slot >= index * slots, 1, 0)
    of_store = lane == store
    row_i = lax.broadcasted_iota(jnp.int32, (group, group), 0)
    row_j = lax.broadcasted_iota(jnp.int32, (group, group), 1)
    earlier = jnp.where(row_j < row_i, 1.0, 0.0).astype(F32)
    rank = jnp.dot(earlier, jnp.where(of_store, 1.0, 0.0).astype(F32), preferred_element_type=F32)
    rank = jnp.sum(jnp.where(of_store, rank, 0.0), axis=1, keepdims=True)
    place = store.astype(F32) * CAP + rank
    home = jnp.where(lane.astype(F32) == place, 1.0, 0.0).astype(F32)
    home = home[:, : stores * CAP]
    outward = home.T.astype(BF16)
    homeward = home.astype(BF16)

    def pack(picked, out):
        packed = jnp.dot(outward, jnp.concatenate(picked, axis=1), preferred_element_type=F32)
        packed = packed.reshape(stores, CAP, tiles * LANES)
        low = packed[:, :, : half * LANES]
        high = packed[:, :, half * LANES :]
        out[...] = jnp.concatenate([low, high], axis=1).astype(BF16)

    def products(taken, deltas):
        results = []
        for k in range(0, tiles, 2):
            x = jnp.concatenate(taken[k : k + 2], axis=0)
            x = jnp.concatenate([jnp.where(m, x, 0.0) for m in own_slot], axis=1)
            w = [deltas[:, k + i].reshape(slots * LANES, LANES) for i in range(2)]
            both = jnp.dot(
                x.astype(BF16), jnp.concatenate(w, axis=1), preferred_element_type=F32
            )
            results += [both[:compact, :LANES], both[compact:, LANES:]]
        return results

    def returned(back):
        got = back[...].astype(F32)
        low = got[:, :CAP].reshape(stores * CAP, half * LANES)
        high = got[:, CAP:].reshape(stores * CAP, half * LANES)
        rows_in = jnp.concatenate([low, high], axis=1).astype(BF16)
        return jnp.dot(homeward, rows_in, preferred_element_type=F32)

    def spread(terms, targets, column):
        total = jnp.where(targets[0] == column, terms[0], 0.0)
        for k in range(1, tiles):
            total += jnp.where(targets[k] == column, terms[k], 0.0)
        return total

    def lanes_of(table, k):
        return jnp.broadcast_to(table[:, k : k + 1], table.shape)

    base_query(0, shards // 4)
    key_copy.start()
    value_copy.start()

    arrive(info_copies)
    where = jnp.zeros((group, LANES), jnp.int32)
    for d in range(stores):
        for s in range(slots):
            where = where + jnp.where(slot == d * slots + s, info[d, s : s + 1, :], 0)
    q_place = [lanes_of(where, k) for k in range(tiles)]
    o_place = [lanes_of(where, tiles + k) for k in range(tiles)]
    head_shift = heads.bit_length() - 1
    tile_shift = all_tiles.bit_length() - 1
    q_source = [lax.shift_right_logical(p, head_shift) for p in q_place]
    o_target = [p & (all_tiles - 1) for p in o_place]

    picked = [jnp.zeros((group, LANES), F32) for _ in range(tiles)]
    for t in range(all_tiles):
        block = act_ref[:, t * LANES : (t + 1) * LANES].astype(F32)
        picked = [jnp.where(q_source[k] == t, block, picked[k]) for k in range(tiles)]
    pack([p.astype(BF16) for p in picked], pack_out)
    pack_in[dp] = pack_out[dp]
    pack_copies = exchange("dp", 1, lambda peer: pack_out.at[peer], pack_in)

    picks = []
    marks = []
    for g in range(stores):
        theirs = info[g, slots : slots + group, :]
        mine = (theirs >= dp * slots) & (theirs < (dp + 1) * slots)
        before = jnp.dot(earlier, jnp.where(mine, 1.0, 0.0), preferred_element_type=F32)
        pick = mine & (lane.astype(F32) == before + g * CAP)
        picks.append(jnp.where(pick, 1.0, 0.0))
        marks.append((theirs - dp * slots + 1).astype(F32))
    expand = jnp.concatenate(picks, axis=0)[:, :compact]
    gather = expand.T
    mark = jnp.dot(gather, jnp.concatenate(marks, axis=0), preferred_element_type=F32)
    expand = expand.astype(BF16)
    gather = gather.astype(BF16)
    own_slot = [mark == s + 1 for s in range(slots)]
    near = jnp.zeros((compact, LANES), jnp.int32)
    one_slot = own_slot
    own_slot = [jnp.concatenate([mark, mark], axis=0) == s + 1 for s in range(slots)]
    for s in range(slots):
        near = near + jnp.where(one_slot[s], info[dp, s : s + 1, :], 0)
    near_target = [lanes_of(near, k) & (heads - 1) for k in range(tiles)]
    near_source = [
        lax.shift_right_logical(lanes_of(near, tiles + k), tile_shift) for k in range(tiles)
    ]

    base_query(shards // 4, 7 * shards // 8)
    od_copy.start()
    start_all(ow_copy)

    qd_copy.wait()
    arrive(pack_copies)
    got = pack_in[...].astype(F32)
    taken = []
    for k in range(tiles):
        start = CAP * (k // half)
        column = (k % half) * LANES
        x = got[:, start : start + CAP, column : column + LANES]
        taken.append(x.reshape(compact, LANES))
    terms = products(taken, qd)
    placed = jnp.concatenate([spread(terms, near_target, h) for h in range(heads)], axis=1)
    placed = jnp.dot(expand, placed.astype(BF16), preferred_element_type=F32)
    placed = placed.reshape(stores, group, width)
    for h in range(heads):
        head_rows[:, :, h, :] = placed[:, :, h * LANES : (h + 1) * LANES]
    extra = head_rows[...].reshape(stores, shards, rows * heads, LANES)
    extra_out[...] = extra.astype(BF16).astype(message)
    extra_in[dp, tp] = extra_out[dp, tp]
    order = [0] + list(range(shards - 1, 0, -1))
    extra_copies = scatter(
        0, lambda to, peer: extra_out.at[to, peer], extra_in, range(shards)
    )

    base_query(7 * shards // 8, shards)
    for h in range(heads):
        head_rows[dp, :, h, :] = acc[:, h * LANES : (h + 1) * LANES]
    q_out[...] = head_rows[dp].reshape(shards, rows * heads, LANES)
    q_in[tp] = q_out[tp]
    q_copies = exchange("tensor", 0, lambda peer: q_out.at[peer], q_in)

    scale = LANES ** (-0.5)
    lines = rows * heads
    line = lax.broadcasted_iota(jnp.int32, (lines, 1), 0)
    of_row = [(line >= r * heads) & (line < (r + 1) * heads) for r in range(rows)]
    limit = jnp.zeros((lines, 1), jnp.int32)
    for r in range(rows):
        limit = jnp.where(of_row[r], length_ref[r], limit)
    visible = lax.broadcasted_iota(jnp.int32, (lines, context), 1) < limit
    kv_heads = keys.shape[1]

    key_copy.wait()
    value_copy.wait()
    arrive(q_copies)

    def attend(step):
        j = peer_of("tensor", step)
        g = j * kv_heads // shards
        q32 = q_in[j]
        for d in range(stores):
            q32 = q32 + extra_in[d, j].astype(F32)
        q32 = q32.astype(BF16).astype(F32)
        fresh_key = jnp.zeros((lines, LANES), F32)
        fresh_value = jnp.zeros((lines, LANES), F32)
        for r in range(rows):
            here = pl.ds(pl.multiple_of(g * LANES, LANES), LANES)
            fresh = fresh_ref[r, :, here].astype(F32)
            fresh_key = jnp.where(of_row[r], fresh[0:1], fresh_key)
            fresh_value = jnp.where(of_row[r], fresh[1:2], fresh_value)
        apart = [jnp.where(of_row[r], q32, 0.0).astype(BF16) for r in range(rows)]
        scores = lax.dot_general(
            jnp.concatenate(apart, axis=1),
            jnp.concatenate([keys[r, g] for r in range(rows)], axis=1),
            (((1,), (1,)), ((), ())),
            preferred_element_type=F32,
        )
        own = jnp.sum(q32 * fresh_key, axis=1, keepdims=True) * scale
        scores = jnp.where(visible, scores * scale, -1e30)
        highest = jnp.maximum(jnp.max(scores, axis=1, keepdims=True), own)
        weights = jnp.where(visible, jnp.exp(scores - highest), 0.0)
        own_weight = jnp.exp(own - highest)
        inverse = 1.0 / (jnp.sum(weights, axis=1, keepdims=True) + own_weight)
        chance = (weights * inverse).astype(BF16)
        own_chance = (own_weight * inverse).astype(BF16).astype(F32)
        side = jnp.concatenate([values[r, g] for r in range(rows)], axis=1)
        side = jnp.dot(chance, side, preferred_element_type=F32)
        mixed = side[:, :LANES]
        for r in range(1, rows):
            mixed = jnp.where(of_row[r], side[:, r * LANES : (r + 1) * LANES], mixed)
        mixed = mixed + own_chance * fresh_value
        a_out[j] = mixed.astype(BF16).astype(message)

    a_copies = {}
    for steps in (order[: shards // 2], order[shards // 2 :]):
        for step in steps:
            source = (shards - step) % shards
            arrive([extra_copies[far, source] for far in range(stores) if far or source])
        for step in steps:
            attend(step)
        a_copies.update(scatter(1, lambda to, peer: a_out.at[peer], a_in, steps))
    a_in[dp, tp] = a_out[tp]

    def pair_copy(c):
        return pltpu.make_async_remote_copy(
            src_ref=pair_out.at[c],
            dst_ref=pair_in.at[c],
            send_sem=pair_send.at[c],
            recv_sem=pair_recv.at[c],
            device_id={"dp": partner, "tensor": lax.rem(tp + c, shards)},
            device_id_type=pl.DeviceIdType.MESH,
        )

    def base_out(first, last):
        def step(c, carry):
            ow_copy(c).wait()
            both = jnp.dot(attended, ow[c], preferred_element_type=F32)
            part[c] = both.reshape(2, group, half_width)
            pair_out[c] = part[c, 1 - parity].astype(BF16)
            pair_copy(c).start()
            return carry

        lax.fori_loop(first, last, step, 0)

    def arrive_from(far):
        for step in range(shards):
            pltpu.make_async_remote_copy(
                src_ref=a_out.at[0],
                dst_ref=a_in.at[dp, tp],
                send_sem=all_send.at[1, far, step],
                recv_sem=all_recv.at[1, far, step],
                device_id={"dp": partner, "tensor": tp},
                device_id_type=pl.DeviceIdType.MESH,
            ).wait_recv()

    near_far = parity + (1 - parity) * (stores - 1)
    arrive([copy for (far, step), copy in a_copies.items() if far == 0])
    arrive_from(near_far)
    pair = pl.ds(dp - parity, 2)
    head_rows[pair] = a_in[pair].astype(F32).reshape(2, group, heads, LANES)
    attended = [head_rows[pair, :, h, :].reshape(2 * group, LANES) for h in range(heads)]
    attended = jnp.concatenate([a.astype(BF16) for a in attended], axis=1)
    base_out(0, shards // 4)
    arrive_from(stores - near_far)
    for far in range(2, stores - 1):
        arrive_from(far)
    head_rows[...] = a_in[...].astype(F32).reshape(stores, group, heads, LANES)
    blocks = [head_rows[:, :, h, :].reshape(stores * group, LANES) for h in range(heads)]
    blocks = jnp.concatenate([b.astype(BF16) for b in blocks], axis=1)
    blocks = jnp.dot(gather, blocks, preferred_element_type=F32)
    taken = []
    for k in range(tiles):
        one = jnp.zeros((compact, LANES), F32)
        for h in range(heads):
            one = jnp.where(near_source[k] == h, blocks[:, h * LANES : (h + 1) * LANES], one)
        taken.append(one)
    od_copy.wait()
    terms = products(taken, od)
    low = jnp.concatenate(terms[:half], axis=1).reshape(stores, CAP, half * LANES)
    high = jnp.concatenate(terms[half:], axis=1).reshape(stores, CAP, half * LANES)
    back_out[...] = jnp.concatenate([low, high], axis=1).astype(BF16)
    back_in[dp] = back_out[dp]
    back_copies = exchange("dp", 2, lambda peer: back_out.at[peer], back_in)
    base_out(shards // 4, shards)
    for copy in sent:
        copy.wait_send()
    arrive(back_copies)
    terms = returned(back_in)
    terms = [terms[:, k * LANES : (k + 1) * LANES] for k in range(tiles)]

    low_half = (1 - parity).astype(F32)
    high_half = parity.astype(F32)

    def whole_part(step):
        owner = peer_of("tensor", step)
        extra = [spread(terms, o_target, owner * heads + h) for h in range(heads)]
        base = part[step, parity]
        return jnp.concatenate(extra, axis=1) + jnp.concatenate(
            [base * low_half, base * high_half], axis=1
        )

    sum_copies = []
    for step in range(1, shards):
        sum_out[step] = whole_part(step).astype(BF16)
        sum_copies.append(send("tensor", 1, step, sum_out.at[step], sum_in.at[step]))
    total = whole_part(0)
    others = jnp.zeros((group, half_width), F32)
    for c in range(shards):
        pair_copy(c).wait_recv()
        others = others + pair_in[c].astype(F32)
    total = total + jnp.concatenate([others * high_half, others * low_half], axis=1)
    for step in range(1, shards):
        sum_copies[step - 1].wait_recv()
        total = total + sum_in[step].astype(F32)
    out_ref[...] = total.astype(BF16)
    for copy in sum_copies:
        copy.wait_send()
    for c in range(shards):
        pair_copy(c).wait_send()


def body(
    activations,
    query_weight,
    output_weight,
    key_cache,
    value_cache,
    fresh_pair,
    cache_length,
    row_tenant,
    tenant_slot,
    query_deltas,
    query_where,
    output_deltas,
    output_where,
):
    stores = lax.axis_size("dp")
    shards = lax.axis_size("tensor")
    group = activations.shape[0]
    rows = key_cache.shape[0]
    width = query_weight.shape[1]
    slots, tiles = query_where.shape
    context = key_cache.shape[2]
    heads = width // LANES
    lines = rows * heads
    message = BF16 if lines % 16 == 0 else F32
    dims = (stores, shards, group, rows, width, tiles, slots, context)
    pack_shape = (stores, 2 * CAP, tiles // 2 * LANES)
    all_shape = (stores, shards, lines, LANES)
    vmem = pl.BlockSpec(memory_space=pltpu.VMEM)
    smem = pl.BlockSpec(memory_space=pltpu.SMEM)
    anywhere = pl.BlockSpec(memory_space=pl.ANY)
    return pl.pallas_call(
        functools.partial(kernel, dims),
        out_shape=jax.ShapeDtypeStruct((group, width), BF16),
        in_specs=[vmem, vmem, smem, smem, smem, vmem, vmem] + [anywhere] * 6,
        out_specs=vmem,
        scratch_shapes=[
            pltpu.VMEM(query_weight.shape, BF16),
            pltpu.VMEM((shards, width, width // 2), BF16),
            pltpu.VMEM(key_cache.shape, BF16),
            pltpu.VMEM(value_cache.shape, BF16),
            pltpu.VMEM(query_deltas.shape, BF16),
            pltpu.VMEM(output_deltas.shape, BF16),
            pltpu.VMEM((stores, slots + group, LANES), jnp.int32),
            pltpu.VMEM((group, width), F32),
            pltpu.VMEM(pack_shape, BF16),
            pltpu.VMEM(pack_shape, BF16),
            pltpu.VMEM(pack_shape, BF16),
            pltpu.VMEM(pack_shape, BF16),
            pltpu.VMEM((stores, group, heads, LANES), F32),
            pltpu.VMEM((shards, lines, LANES), F32),
            pltpu.VMEM((shards, lines, LANES), F32),
            pltpu.VMEM(all_shape, message),
            pltpu.VMEM(all_shape, message),
            pltpu.VMEM((shards, lines, LANES), message),
            pltpu.VMEM(all_shape, message),
            pltpu.VMEM((shards, 2, group, width // 2), F32),
            pltpu.VMEM((shards, group, width), BF16),
            pltpu.VMEM((shards, group, width), BF16),
            pltpu.SemaphoreType.DMA((shards,)),
            pltpu.SemaphoreType.DMA((shards,)),
            pltpu.SemaphoreType.DMA((2,)),
            pltpu.SemaphoreType.DMA((2,)),
            pltpu.SemaphoreType.DMA((3, stores)),
            pltpu.SemaphoreType.DMA((3, stores)),
            pltpu.SemaphoreType.DMA((2, shards)),
            pltpu.SemaphoreType.DMA((2, shards)),
            pltpu.SemaphoreType.DMA((2, stores, shards)),
            pltpu.SemaphoreType.DMA((2, stores, shards)),
            pltpu.VMEM((shards, group, width // 2), BF16),
            pltpu.VMEM((shards, group, width // 2), BF16),
            pltpu.SemaphoreType.DMA((shards,)),
            pltpu.SemaphoreType.DMA((shards,)),
        ],
        compiler_params=pltpu.CompilerParams(
            collective_id=0, has_side_effects=True, vmem_limit_bytes=56 * 1024 * 1024
        ),
        name="decode_layer",
    )(
        activations,
        fresh_pair,
        cache_length,
        row_tenant,
        tenant_slot,
        query_where,
        output_where,
        query_weight,
        output_weight,
        key_cache,
        value_cache,
        query_deltas,
        output_deltas,
    )


def solution(mesh):
    placed = (
        P("dp", None),
        P(None, "tensor"),
        P("tensor", None),
        P(("dp", "tensor"), None, None, None),
        P(("dp", "tensor"), None, None, None),
        P(("dp", "tensor"), None, None),
        P(("dp", "tensor")),
        P("dp"),
        P(),
        P("dp", "tensor", None, None),
        P("dp", "tensor"),
        P("dp", "tensor", None, None),
        P("dp", "tensor"),
    )
    return jax.shard_map(
        body, mesh=mesh, in_specs=placed, out_specs=P("dp", "tensor"), check_vma=False
    )
```

```python
import functools

import jax
import jax.numpy as jnp
from jax import lax
from jax.experimental import pallas as pl
from jax.experimental.pallas import tpu as pltpu
from jax.sharding import PartitionSpec as P

LANES = 128
CAP = 8
F32 = jnp.float32
BF16 = jnp.bfloat16


def kernel(
    dims,
    act_ref,
    fresh_ref,
    length_ref,
    tenant_ref,
    table_ref,
    qwhere_ref,
    owhere_ref,
    qw_hbm,
    ow_hbm,
    key_hbm,
    value_hbm,
    qd_hbm,
    od_hbm,
    out_ref,
    qw,
    ow,
    keys,
    values,
    qd,
    od,
    info,
    acc,
    pack_out,
    pack_in,
    back_out,
    back_in,
    head_rows,
    q_out,
    q_in,
    extra_out,
    extra_in,
    a_out,
    a_in,
    part,
    sum_out,
    sum_in,
    qw_sem,
    ow_sem,
    cache_sem,
    delta_sem,
    dp_send,
    dp_recv,
    tp_send,
    tp_recv,
    all_send,
    all_recv,
    pair_out,
    pair_in,
    pair_send,
    pair_recv,
):
    stores, shards, group, rows, width, tiles, slots, context = dims
    heads = width // LANES
    all_tiles = act_ref.shape[1] // LANES
    half = tiles // 2
    dp = lax.axis_index("dp")
    tp = lax.axis_index("tensor")
    chunk = qw.shape[0] // shards
    message = a_out.dtype
    compact = stores * CAP
    half_width = width // 2
    parity = lax.rem(dp, 2)
    partner = dp + 1 - 2 * parity

    peers = {
        "dp": [dp] + [lax.rem(dp + step, stores) for step in range(1, stores)],
        "tensor": [tp] + [lax.rem(tp + step, shards) for step in range(1, shards)],
    }

    def peer_of(axis, step):
        return peers[axis][step]

    qd_copy = pltpu.make_async_copy(qd_hbm, qd, delta_sem.at[0])
    od_copy = pltpu.make_async_copy(od_hbm, od, delta_sem.at[1])
    key_copy = pltpu.make_async_copy(key_hbm, keys, cache_sem.at[0])
    value_copy = pltpu.make_async_copy(value_hbm, values, cache_sem.at[1])

    def qw_copy(c):
        span = pl.ds(pl.multiple_of(c * chunk, chunk), chunk)
        return pltpu.make_async_copy(qw_hbm.at[span], qw.at[span], qw_sem.at[c])

    def ow_copy(c):
        owner = lax.rem(tp + c, shards)
        start = owner * width + parity * half_width
        span = pl.ds(pl.multiple_of(start, half_width), half_width)
        return pltpu.make_async_copy(ow_hbm.at[:, span], ow.at[c], ow_sem.at[c])

    def start_all(copy):
        def step(c, carry):
            copy(c).start()
            return carry

        lax.fori_loop(0, shards, step, 0)

    barrier = pltpu.get_barrier_semaphore()
    for axis in ("dp", "tensor"):
        for peer in peers[axis][1:]:
            pl.semaphore_signal(
                barrier, inc=1, device_id={axis: peer}, device_id_type=pl.DeviceIdType.MESH
            )
    start_all(qw_copy)
    qd_copy.start()

    lane = lax.broadcasted_iota(jnp.int32, (group, LANES), 1)
    row = lax.broadcasted_iota(jnp.int32, (group, LANES), 0)
    slot = jnp.zeros((group, LANES), jnp.int32)
    for r in range(group):
        slot = jnp.where(row == r, table_ref[tenant_ref[r]], slot)
    info[dp] = jnp.zeros(info.shape[1:], jnp.int32)
    info[dp, 0:slots, 0:tiles] = qwhere_ref[...]
    info[dp, 0:slots, tiles : 2 * tiles] = owhere_ref[...]
    info[dp, slots : slots + group, :] = slot
    acc[...] = jnp.zeros_like(acc)
    pl.semaphore_wait(barrier, stores - 1 + shards - 1)

    def send(axis, phase, step, src, dst):
        sems = (dp_send, dp_recv) if axis == "dp" else (tp_send, tp_recv)
        copy = pltpu.make_async_remote_copy(
            src_ref=src,
            dst_ref=dst,
            send_sem=sems[0].at[phase, step],
            recv_sem=sems[1].at[phase, step],
            device_id={axis: peer_of(axis, step)},
            device_id_type=pl.DeviceIdType.MESH,
        )
        copy.start()
        return copy

    sent = []

    def exchange(axis, phase, src, dst):
        me, count = (dp, stores) if axis == "dp" else (tp, shards)
        copies = [
            send(axis, phase, step, src(peer_of(axis, step)), dst.at[me])
            for step in range(1, count)
        ]
        sent.extend(copies)
        return copies

    def scatter(phase, src, dst, steps):
        copies = {}
        for step in steps:
            peer = peer_of("tensor", step)
            for far in reversed(range(stores)):
                if step == 0 and far == 0:
                    continue
                to = peer_of("dp", far)
                copy = pltpu.make_async_remote_copy(
                    src_ref=src(to, peer),
                    dst_ref=dst.at[dp, tp],
                    send_sem=all_send.at[phase, far, step],
                    recv_sem=all_recv.at[phase, far, step],
                    device_id={"dp": to, "tensor": peer},
                    device_id_type=pl.DeviceIdType.MESH,
                )
                copy.start()
                copies[far, step] = copy
        sent.extend(copies.values())
        return copies

    def arrive(copies):
        for copy in copies:
            copy.wait_recv()

    info_copies = exchange("dp", 0, lambda peer: info.at[dp], info)

    def base_query(first, last):
        def step(c, carry):
            qw_copy(c).wait()
            span = pl.ds(pl.multiple_of(c * chunk, chunk), chunk)
            acc[...] += jnp.dot(act_ref[:, span], qw[span, :], preferred_element_type=F32)
            return carry

        lax.fori_loop(first, last, step, 0)

    store = jnp.zeros((group, LANES), jnp.int32)
    for index in range(1, stores):
        store = store + jnp.where(slot >= index * slots, 1, 0)
    of_store = lane == store
    row_i = lax.broadcasted_iota(jnp.int32, (group, group), 0)
    row_j = lax.broadcasted_iota(jnp.int32, (group, group), 1)
    earlier = jnp.where(row_j < row_i, 1.0, 0.0).astype(F32)
    rank = jnp.dot(earlier, jnp.where(of_store, 1.0, 0.0).astype(F32), preferred_element_type=F32)
    rank = jnp.sum(jnp.where(of_store, rank, 0.0), axis=1, keepdims=True)
    place = store.astype(F32) * CAP + rank
    home = jnp.where(lane.astype(F32) == place, 1.0, 0.0).astype(F32)
    home = home[:, : stores * CAP]
    outward = home.T.astype(BF16)
    homeward = home.astype(BF16)

    def pack(picked, out):
        packed = jnp.dot(outward, jnp.concatenate(picked, axis=1), preferred_element_type=F32)
        packed = packed.reshape(stores, CAP, tiles * LANES)
        low = packed[:, :, : half * LANES]
        high = packed[:, :, half * LANES :]
        out[...] = jnp.concatenate([low, high], axis=1).astype(BF16)

    def products(taken, deltas):
        results = []
        for k in range(tiles):
            x = jnp.concatenate([jnp.where(m, taken[k], 0.0) for m in own_slot], axis=1)
            w = deltas[:, k].reshape(slots * LANES, LANES)
            results.append(jnp.dot(x.astype(BF16), w, preferred_element_type=F32))
        return results

    def returned(back):
        got = back[...].astype(F32)
        low = got[:, :CAP].reshape(stores * CAP, half * LANES)
        high = got[:, CAP:].reshape(stores * CAP, half * LANES)
        rows_in = jnp.concatenate([low, high], axis=1).astype(BF16)
        return jnp.dot(homeward, rows_in, preferred_element_type=F32)

    def spread(terms, targets, column):
        total = jnp.where(targets[0] == column, terms[0], 0.0)
        for k in range(1, tiles):
            total += jnp.where(targets[k] == column, terms[k], 0.0)
        return total

    def lanes_of(table, k):
        return jnp.broadcast_to(table[:, k : k + 1], table.shape)

    base_query(0, shards // 4)
    key_copy.start()
    value_copy.start()

    arrive(info_copies)
    where = jnp.zeros((group, LANES), jnp.int32)
    for d in range(stores):
        for s in range(slots):
            where = where + jnp.where(slot == d * slots + s, info[d, s : s + 1, :], 0)
    q_place = [lanes_of(where, k) for k in range(tiles)]
    o_place = [lanes_of(where, tiles + k) for k in range(tiles)]
    head_shift = heads.bit_length() - 1
    tile_shift = all_tiles.bit_length() - 1
    q_source = [lax.shift_right_logical(p, head_shift) for p in q_place]
    o_target = [p & (all_tiles - 1) for p in o_place]

    picked = [jnp.zeros((group, LANES), F32) for _ in range(tiles)]
    for t in range(all_tiles):
        block = act_ref[:, t * LANES : (t + 1) * LANES].astype(F32)
        picked = [jnp.where(q_source[k] == t, block, picked[k]) for k in range(tiles)]
    pack([p.astype(BF16) for p in picked], pack_out)
    pack_in[dp] = pack_out[dp]
    pack_copies = exchange("dp", 1, lambda peer: pack_out.at[peer], pack_in)

    picks = []
    marks = []
    for g in range(stores):
        theirs = info[g, slots : slots + group, :]
        mine = (theirs >= dp * slots) & (theirs < (dp + 1) * slots)
        before = jnp.dot(earlier, jnp.where(mine, 1.0, 0.0), preferred_element_type=F32)
        pick = mine & (lane.astype(F32) == before + g * CAP)
        picks.append(jnp.where(pick, 1.0, 0.0))
        marks.append((theirs - dp * slots + 1).astype(F32))
    expand = jnp.concatenate(picks, axis=0)[:, :compact]
    gather = expand.T
    mark = jnp.dot(gather, jnp.concatenate(marks, axis=0), preferred_element_type=F32)
    expand = expand.astype(BF16)
    gather = gather.astype(BF16)
    own_slot = [mark == s + 1 for s in range(slots)]
    near = jnp.zeros((compact, LANES), jnp.int32)
    for s in range(slots):
        near = near + jnp.where(own_slot[s], info[dp, s : s + 1, :], 0)
    near_target = [lanes_of(near, k) & (heads - 1) for k in range(tiles)]
    near_source = [
        lax.shift_right_logical(lanes_of(near, tiles + k), tile_shift) for k in range(tiles)
    ]

    base_query(shards // 4, shards)
    od_copy.start()
    start_all(ow_copy)
    for h in range(heads):
        head_rows[dp, :, h, :] = acc[:, h * LANES : (h + 1) * LANES]
    q_out[...] = head_rows[dp].reshape(shards, rows * heads, LANES)
    q_in[tp] = q_out[tp]
    q_copies = exchange("tensor", 0, lambda peer: q_out.at[peer], q_in)


    qd_copy.wait()
    arrive(pack_copies)
    got = pack_in[...].astype(F32)
    taken = []
    for k in range(tiles):
        start = CAP * (k // half)
        column = (k % half) * LANES
        x = got[:, start : start + CAP, column : column + LANES]
        taken.append(x.reshape(compact, LANES))
    terms = products(taken, qd)
    placed = jnp.concatenate([spread(terms, near_target, h) for h in range(heads)], axis=1)
    placed = jnp.dot(expand, placed.astype(BF16), preferred_element_type=F32)
    placed = placed.reshape(stores, group, width)
    for h in range(heads):
        head_rows[:, :, h, :] = placed[:, :, h * LANES : (h + 1) * LANES]
    extra = head_rows[...].reshape(stores, shards, rows * heads, LANES)
    extra_out[...] = extra.astype(BF16).astype(message)
    extra_in[dp, tp] = extra_out[dp, tp]
    order = [0] + list(range(shards - 1, 0, -1))
    extra_copies = scatter(
        0, lambda to, peer: extra_out.at[to, peer], extra_in, range(shards)
    )

    scale = LANES ** (-0.5)
    lines = rows * heads
    line = lax.broadcasted_iota(jnp.int32, (lines, 1), 0)
    of_row = [(line >= r * heads) & (line < (r + 1) * heads) for r in range(rows)]
    limit = jnp.zeros((lines, 1), jnp.int32)
    for r in range(rows):
        limit = jnp.where(of_row[r], length_ref[r], limit)
    visible = lax.broadcasted_iota(jnp.int32, (lines, context), 1) < limit
    kv_heads = keys.shape[1]

    key_copy.wait()
    value_copy.wait()
    arrive(q_copies)

    def attend(step):
        j = peer_of("tensor", step)
        g = j * kv_heads // shards
        q32 = q_in[j]
        for d in range(stores):
            q32 = q32 + extra_in[d, j].astype(F32)
        q = q32.astype(BF16)
        q32 = q.astype(F32)
        fresh_key = jnp.zeros((lines, LANES), F32)
        fresh_value = jnp.zeros((lines, LANES), F32)
        scores = None
        for r in range(rows):
            here = pl.ds(pl.multiple_of(g * LANES, LANES), LANES)
            fresh = fresh_ref[r, :, here].astype(F32)
            fresh_key = jnp.where(of_row[r], fresh[0:1], fresh_key)
            fresh_value = jnp.where(of_row[r], fresh[1:2], fresh_value)
            one = lax.dot_general(
                q, keys[r, g], (((1,), (1,)), ((), ())), preferred_element_type=F32
            )
            scores = one if scores is None else jnp.where(of_row[r], one, scores)
        own = jnp.sum(q32 * fresh_key, axis=1, keepdims=True) * scale
        scores = jnp.where(visible, scores * scale, -1e30)
        highest = jnp.maximum(jnp.max(scores, axis=1, keepdims=True), own)
        weights = jnp.where(visible, jnp.exp(scores - highest), 0.0)
        own_weight = jnp.exp(own - highest)
        inverse = 1.0 / (jnp.sum(weights, axis=1, keepdims=True) + own_weight)
        chance = (weights * inverse).astype(BF16)
        own_chance = (own_weight * inverse).astype(BF16).astype(F32)
        mixed = None
        for r in range(rows):
            one = jnp.dot(chance, values[r, g], preferred_element_type=F32)
            mixed = one if mixed is None else jnp.where(of_row[r], one, mixed)
        mixed = mixed + own_chance * fresh_value
        a_out[j] = mixed.astype(BF16).astype(message)

    a_copies = {}
    for steps in (order[: shards // 2], order[shards // 2 :]):
        for step in steps:
            source = (shards - step) % shards
            arrive([extra_copies[far, source] for far in range(stores) if far or source])
        for step in steps:
            attend(step)
        a_copies.update(scatter(1, lambda to, peer: a_out.at[peer], a_in, steps))
    a_in[dp, tp] = a_out[tp]

    def pair_copy(c):
        return pltpu.make_async_remote_copy(
            src_ref=pair_out.at[c],
            dst_ref=pair_in.at[c],
            send_sem=pair_send.at[c],
            recv_sem=pair_recv.at[c],
            device_id={"dp": partner, "tensor": lax.rem(tp + c, shards)},
            device_id_type=pl.DeviceIdType.MESH,
        )

    def base_out(first, last):
        def step(c, carry):
            ow_copy(c).wait()
            both = jnp.dot(attended, ow[c], preferred_element_type=F32)
            part[c] = both.reshape(2, group, half_width)
            pair_out[c] = part[c, 1 - parity].astype(BF16)
            pair_copy(c).start()
            return carry

        lax.fori_loop(first, last, step, 0)

    def arrive_from(far):
        for step in range(shards):
            pltpu.make_async_remote_copy(
                src_ref=a_out.at[0],
                dst_ref=a_in.at[dp, tp],
                send_sem=all_send.at[1, far, step],
                recv_sem=all_recv.at[1, far, step],
                device_id={"dp": partner, "tensor": tp},
                device_id_type=pl.DeviceIdType.MESH,
            ).wait_recv()

    near_far = parity + (1 - parity) * (stores - 1)
    arrive([copy for (far, step), copy in a_copies.items() if far == 0])
    arrive_from(near_far)
    pair = pl.ds(dp - parity, 2)
    head_rows[pair] = a_in[pair].astype(F32).reshape(2, group, heads, LANES)
    attended = [head_rows[pair, :, h, :].reshape(2 * group, LANES) for h in range(heads)]
    attended = jnp.concatenate([a.astype(BF16) for a in attended], axis=1)
    base_out(0, shards // 4)
    arrive_from(stores - near_far)
    for far in range(2, stores - 1):
        arrive_from(far)
    head_rows[...] = a_in[...].astype(F32).reshape(stores, group, heads, LANES)
    blocks = [head_rows[:, :, h, :].reshape(stores * group, LANES) for h in range(heads)]
    blocks = jnp.concatenate([b.astype(BF16) for b in blocks], axis=1)
    blocks = jnp.dot(gather, blocks, preferred_element_type=F32)
    taken = []
    for k in range(tiles):
        one = jnp.zeros((compact, LANES), F32)
        for h in range(heads):
            one = jnp.where(near_source[k] == h, blocks[:, h * LANES : (h + 1) * LANES], one)
        taken.append(one)
    od_copy.wait()
    terms = products(taken, od)
    low = jnp.concatenate(terms[:half], axis=1).reshape(stores, CAP, half * LANES)
    high = jnp.concatenate(terms[half:], axis=1).reshape(stores, CAP, half * LANES)
    back_out[...] = jnp.concatenate([low, high], axis=1).astype(BF16)
    back_in[dp] = back_out[dp]
    back_copies = exchange("dp", 2, lambda peer: back_out.at[peer], back_in)
    base_out(shards // 4, shards)
    for copy in sent:
        copy.wait_send()
    arrive(back_copies)
    terms = returned(back_in)
    terms = [terms[:, k * LANES : (k + 1) * LANES] for k in range(tiles)]

    low_half = (1 - parity).astype(F32)
    high_half = parity.astype(F32)

    def whole_part(step):
        owner = peer_of("tensor", step)
        extra = [spread(terms, o_target, owner * heads + h) for h in range(heads)]
        base = part[step, parity]
        return jnp.concatenate(extra, axis=1) + jnp.concatenate(
            [base * low_half, base * high_half], axis=1
        )

    sum_copies = []
    for step in range(1, shards):
        sum_out[step] = whole_part(step).astype(BF16)
        sum_copies.append(send("tensor", 1, step, sum_out.at[step], sum_in.at[step]))
    total = whole_part(0)
    others = jnp.zeros((group, half_width), F32)
    for c in range(shards):
        pair_copy(c).wait_recv()
        others = others + pair_in[c].astype(F32)
    total = total + jnp.concatenate([others * high_half, others * low_half], axis=1)
    for step in range(1, shards):
        sum_copies[step - 1].wait_recv()
        total = total + sum_in[step].astype(F32)
    out_ref[...] = total.astype(BF16)
    for copy in sum_copies:
        copy.wait_send()
    for c in range(shards):
        pair_copy(c).wait_send()


def body(
    activations,
    query_weight,
    output_weight,
    key_cache,
    value_cache,
    fresh_pair,
    cache_length,
    row_tenant,
    tenant_slot,
    query_deltas,
    query_where,
    output_deltas,
    output_where,
):
    stores = lax.axis_size("dp")
    shards = lax.axis_size("tensor")
    group = activations.shape[0]
    rows = key_cache.shape[0]
    width = query_weight.shape[1]
    slots, tiles = query_where.shape
    context = key_cache.shape[2]
    heads = width // LANES
    lines = rows * heads
    message = BF16 if lines % 16 == 0 else F32
    dims = (stores, shards, group, rows, width, tiles, slots, context)
    pack_shape = (stores, 2 * CAP, tiles // 2 * LANES)
    all_shape = (stores, shards, lines, LANES)
    vmem = pl.BlockSpec(memory_space=pltpu.VMEM)
    smem = pl.BlockSpec(memory_space=pltpu.SMEM)
    anywhere = pl.BlockSpec(memory_space=pl.ANY)
    return pl.pallas_call(
        functools.partial(kernel, dims),
        out_shape=jax.ShapeDtypeStruct((group, width), BF16),
        in_specs=[vmem, vmem, smem, smem, smem, vmem, vmem] + [anywhere] * 6,
        out_specs=vmem,
        scratch_shapes=[
            pltpu.VMEM(query_weight.shape, BF16),
            pltpu.VMEM((shards, width, width // 2), BF16),
            pltpu.VMEM(key_cache.shape, BF16),
            pltpu.VMEM(value_cache.shape, BF16),
            pltpu.VMEM(query_deltas.shape, BF16),
            pltpu.VMEM(output_deltas.shape, BF16),
            pltpu.VMEM((stores, slots + group, LANES), jnp.int32),
            pltpu.VMEM((group, width), F32),
            pltpu.VMEM(pack_shape, BF16),
            pltpu.VMEM(pack_shape, BF16),
            pltpu.VMEM(pack_shape, BF16),
            pltpu.VMEM(pack_shape, BF16),
            pltpu.VMEM((stores, group, heads, LANES), F32),
            pltpu.VMEM((shards, lines, LANES), F32),
            pltpu.VMEM((shards, lines, LANES), F32),
            pltpu.VMEM(all_shape, message),
            pltpu.VMEM(all_shape, message),
            pltpu.VMEM((shards, lines, LANES), message),
            pltpu.VMEM(all_shape, message),
            pltpu.VMEM((shards, 2, group, width // 2), F32),
            pltpu.VMEM((shards, group, width), BF16),
            pltpu.VMEM((shards, group, width), BF16),
            pltpu.SemaphoreType.DMA((shards,)),
            pltpu.SemaphoreType.DMA((shards,)),
            pltpu.SemaphoreType.DMA((2,)),
            pltpu.SemaphoreType.DMA((2,)),
            pltpu.SemaphoreType.DMA((3, stores)),
            pltpu.SemaphoreType.DMA((3, stores)),
            pltpu.SemaphoreType.DMA((2, shards)),
            pltpu.SemaphoreType.DMA((2, shards)),
            pltpu.SemaphoreType.DMA((2, stores, shards)),
            pltpu.SemaphoreType.DMA((2, stores, shards)),
            pltpu.VMEM((shards, group, width // 2), BF16),
            pltpu.VMEM((shards, group, width // 2), BF16),
            pltpu.SemaphoreType.DMA((shards,)),
            pltpu.SemaphoreType.DMA((shards,)),
        ],
        compiler_params=pltpu.CompilerParams(
            collective_id=0, has_side_effects=True, vmem_limit_bytes=56 * 1024 * 1024
        ),
        name="decode_layer",
    )(
        activations,
        fresh_pair,
        cache_length,
        row_tenant,
        tenant_slot,
        query_where,
        output_where,
        query_weight,
        output_weight,
        key_cache,
        value_cache,
        query_deltas,
        output_deltas,
    )


def solution(mesh):
    placed = (
        P("dp", None),
        P(None, "tensor"),
        P("tensor", None),
        P(("dp", "tensor"), None, None, None),
        P(("dp", "tensor"), None, None, None),
        P(("dp", "tensor"), None, None),
        P(("dp", "tensor")),
        P("dp"),
        P(),
        P("dp", "tensor", None, None),
        P("dp", "tensor"),
        P("dp", "tensor", None, None),
        P("dp", "tensor"),
    )
    return jax.shard_map(
        body, mesh=mesh, in_specs=placed, out_specs=P("dp", "tensor"), check_vma=False
    )
```
